256 devices in a mesh: dp: 2 (over x_lo), row: 8 (over y, core), col: 16 (over z, x_hi).
Axes of the slice: x: 4 (x_hi: 2, x_lo: 2; x = x_hi * 2 + x_lo), y: 4, z: 8, core: 2. Of those that a mesh axis runs over, the one named last changes fastest.
Arguments:
- inputs: bfloat16 [1280, 12288], P(('dp', 'row'), 'col'), may hold values from -3 to 3
- upstream: bfloat16 [1280, 12288], P(('dp', 'row'), 'col'), may hold values from -3 to 3
- preact: bfloat16 [1280, 2, 12288], P(('dp', 'col'), None, 'row'), may hold values from -5 to 5
- w_in: bfloat16 [12288, 2, 12288], P('col', 'dp', 'row'), may hold values from -0.0546875 to 0.0546875
- w_out: bfloat16 [2, 12288, 12288], P('dp', 'row', 'col'), may hold values from -0.0390625 to 0.0390625
Outputs:
- grad_in: bfloat16 [1280, 12288], P(('dp', 'row'), 'col')
- grad_w_in: bfloat16 [12288, 2, 12288], P('col', 'dp', 'row')
- grad_w_out: bfloat16 [2, 12288, 12288], P('dp', 'row', 'col')
The draws below stay inside these ranges and needn't reach their ends.
All inputs are finite; a program needn't handle non-finite values.
Results may differ from the reference program's by a relative error of at most 0.006.
Values may be sent and summed in bfloat16 or wider, within the bound.
A program may use at most 128 MiB of HBM per device.

```python
import jax
import jax.numpy as jnp
from jax import lax

D = 12288
HID = 24576
TOK = 640
FH = 12288
TOKENS = 1280
N_DP = 2


def shard_levels(key, shape, pieces, least, high):
    level, own = 1.0, jax.random.fold_in(key, 6)
    for axis_at, parts in pieces:
        heights = jnp.exp(jax.random.uniform(jax.random.fold_in(own, axis_at), (parts,), jnp.float32, least / len(pieces), high / len(pieces)))
        level = level * jnp.repeat(heights, shape[axis_at] // parts).reshape([-1 if axis == axis_at else 1 for axis in range(len(shape))])
    return level


def scatter_about(stream_key, shape, scale, reach, split=(), kind=jnp.bfloat16):
    drawn = scale * jax.random.normal(stream_key, shape, jnp.float32)
    if split:
        drawn = drawn * shard_levels(stream_key, shape, split, -0.22, 0.18)
    return jnp.clip(drawn, -reach, reach).astype(kind)


def setup_inputs(seed: int = 0) -> dict:
    seeds = jax.random.split(jax.random.key(seed), 6)
    return {
        "inputs": scatter_about(seeds[0], (TOKENS, D), 0.5, 3.0, ((0, 16), (1, 16))),
        "upstream": scatter_about(seeds[1], (TOKENS, D), 0.5, 3.0, ((0, 16), (1, 16))),
        "preact": scatter_about(seeds[2], (TOKENS, N_DP, FH), 1.0, 5.0, ((0, 32), (2, 8))),
        "w_in": scatter_about(seeds[3], (D, N_DP, FH), D ** -0.5, 0.0546875, ((0, 16), (1, 2), (2, 8))),
        "w_out": scatter_about(seeds[4], (N_DP, FH, D), HID ** -0.5, 0.0390625, ((0, 2), (1, 8), (2, 16))),
    }


GELU_C = 0.7978845608028654
GELU_K = 0.044715


def gelu_parts(values):
    wide = values.astype(jnp.float32)
    inner = jnp.tanh(GELU_C * (wide + GELU_K * wide * wide * wide))
    active = 0.5 * wide * (1.0 + inner)
    slope = 0.5 * (1.0 + inner) + 0.5 * wide * (1.0 - inner * inner) * GELU_C * (1.0 + 3.0 * GELU_K * wide * wide)
    return active, slope


def reference(inputs, upstream, preact, w_in, w_out):
    w_in_mat = w_in.reshape(D, HID)
    w_out_mat = w_out.reshape(HID, D)
    pre_mat = preact.reshape(TOKENS, HID)
    back = jnp.dot(upstream, w_out_mat.T, preferred_element_type=jnp.float32)
    active, slope = gelu_parts(pre_mat)
    grad_pre = (back * slope).astype(jnp.bfloat16)
    act_low = active.astype(jnp.bfloat16)
    grad_in = jnp.dot(grad_pre, w_in_mat.T, preferred_element_type=jnp.float32).astype(jnp.bfloat16)
    total_in = jnp.zeros((D, HID), jnp.float32)
    total_out = jnp.zeros((HID, D), jnp.float32)
    for replica in range(N_DP):
        lower = replica * TOK
        part_in = jnp.dot(inputs[lower:lower + TOK].T, grad_pre[lower:lower + TOK], preferred_element_type=jnp.float32)
        total_in = total_in + lax.optimization_barrier(part_in.astype(jnp.bfloat16)).astype(jnp.float32)
        part_out = jnp.dot(act_low[lower:lower + TOK].T, upstream[lower:lower + TOK], preferred_element_type=jnp.float32)
        total_out = total_out + lax.optimization_barrier(part_out.astype(jnp.bfloat16)).astype(jnp.float32)
    grad_w_in = total_in.astype(jnp.bfloat16).reshape(D, N_DP, FH)
    grad_w_out = total_out.astype(jnp.bfloat16).reshape(N_DP, FH, D)
    return grad_in, grad_w_in, grad_w_out
```

```python
import functools

import jax
import jax.numpy as jnp
from jax import lax
from jax.experimental import pallas as pl
from jax.experimental.pallas import tpu as pltpu
from jax.sharding import PartitionSpec as P

GELU_C = 0.7978845608028654
GELU_K = 0.044715
MESH = pl.DeviceIdType.MESH
BF = jnp.bfloat16
F32 = jnp.float32

B = 80
D = 768
H = 1536
HA = 768
HB = H - HA
HD = D // 2
SIGN = (1, -1)


def gelu_parts(wide):
    inner = jnp.tanh(GELU_C * (wide + GELU_K * wide * wide * wide))
    active = 0.5 * wide * (1.0 + inner)
    slope = 0.5 * (1.0 + inner) + 0.5 * wide * (1.0 - inner * inner) * GELU_C * (
        1.0 + 3.0 * GELU_K * wide * wide
    )
    return active, slope


def dot(a, b, ca, cb):
    return lax.dot_general(a, b, (((ca,), (cb,)), ((), ())), preferred_element_type=F32)


def cols_of(lane):
    return pl.ds(0, HA) if lane < 2 else pl.ds(HA, HB)


def half_of(lane, part):
    if lane < 2:
        return pl.ds(part * (HA // 2), HA // 2)
    return pl.ds(HA + part * (HB // 2), HB // 2)


def kernel(
    inp, ups, pre, w_in, w_out,
    gin_o, gwin_o, gwout_o,
    UI, AG, PB, WI, WO, PRE, SL, RA, SA, RB, SB, XBr, XBs, XA, CS, Q, GO, GI, PO, PI,
    w_sem, o_sem, p_r, p_s, u_r, u_s, u_f, z_r, z_s, xa_r, xa_s, xb_r, xb_s,
    rz_r, rz_s, rxb_r, rxb_s, rxa, cs_r, cs_s, gi_r, gi_s,
):
    dp, row, col = lax.axis_index("dp"), lax.axis_index("row"), lax.axis_index("col")
    y, core = lax.div(row, 2), lax.rem(row, 2)
    z, xh = lax.div(col, 2), lax.rem(col, 2)
    xo = 1 - xh
    me_d = dp * 8 + row
    chip_d = dp * 4 + y
    n_me = xh * 8 + z

    def zrel(d):
        return lax.rem(z + (d + 8), 8)

    def blk(lane, d):
        return (xo if lane == 1 else xh) * 8 + zrel(d)

    nbr = tuple((dp, row, zrel(s) * 2 + xh) for s in SIGN)
    partner = (dp, row, z * 2 + xo)
    sib = (dp, y * 2 + (1 - core), col)

    def rc(src, dst, ss, rs, dev):
        return pltpu.make_async_remote_copy(
            src_ref=src, dst_ref=dst, send_sem=ss, recv_sem=rs, device_id=dev, device_id_type=MESH
        )

    def got(ref, sem):
        pltpu.make_async_copy(ref, ref, sem).wait()

    wcopy_out = pltpu.make_async_copy(w_out, WO, w_sem.at[0])
    wcopy_in = pltpu.make_async_copy(w_in, WI, w_sem.at[1])
    wcopy_out.start()
    wcopy_in.start()

    barrier = pltpu.get_barrier_semaphore()

    def greet(dev):
        pl.semaphore_signal(barrier, inc=1, device_id=dev, device_id_type=MESH)

    def greet_group(j, _):
        t = lax.rem(me_d + j, 16)
        greet((lax.div(t, 8), lax.rem(t, 8), col))
        return 0

    lax.fori_loop(1, 16, greet_group, 0)
    greet(nbr[0])
    greet(nbr[1])
    greet(partner)
    greet((1 - dp, row, z * 2 + xo))
    UI[0, me_d] = ups[...]
    UI[1, me_d] = inp[...]
    pl.semaphore_wait(barrier, 19)

    def feature_start(a):
        own = UI.at[a, me_d]

        def send(j, _):
            t = lax.rem(chip_d + j, 8)
            dev = (lax.div(t, 4), lax.rem(t, 4) * 2 + core, col)
            rc(own, own, u_s.at[a, j], u_r.at[a, me_d], dev).start()
            return 0

        lax.fori_loop(1, 8, send, 0)
        rc(own, own, u_f.at[a, 0], u_r.at[a, me_d], sib).start()

    def feature_pass(a):
        def step(j, _):
            t = lax.rem(chip_d + 8 - j, 8)
            n = lax.div(t, 4) * 8 + lax.rem(t, 4) * 2 + core
            ref = UI.at[a, n]
            got(ref, u_r.at[a, n])
            rc(ref, ref, u_f.at[a, j], u_r.at[a, n], sib).start()
            return 0

        lax.fori_loop(1, 8, step, 0)

    def feature_end(a):
        def step(j, _):
            n = j * 2 + (1 - core)
            got(UI.at[a, n], u_r.at[a, n])
            return 0

        lax.fori_loop(0, 8, step, 0)

    feature_start(0)

    for k in range(2):
        own = jnp.logical_and(dp == k, dp == xh)
        src, dst = pre.at[k], PRE.at[xh]

        @pl.when(own)
        def _():
            pltpu.make_async_copy(src, dst, p_r.at[xh]).start()

        @pl.when(jnp.logical_not(own))
        def _():
            rc(src, dst, p_s.at[k], p_r.at[xh], (k, row, z * 2 + dp)).start()

    feature_start(1)

    got(PRE.at[0], p_r.at[0])
    got(PRE.at[1], p_r.at[1])
    wide = jnp.concatenate([PRE[0].astype(F32)[:40], PRE[1].astype(F32)[:40]], axis=0)
    active, slope = gelu_parts(wide)
    AG[0, n_me] = active.astype(BF)
    SL[...] = slope

    def z_send(a, di, h, lane, d):
        cols = cols_of(lane) if h < 4 else half_of(lane, di)
        ref = AG.at[a, blk(lane, d), :, cols]
        rc(ref, ref, z_s.at[a, di, h - 1, lane], z_r.at[a, di, h - 1, lane], nbr[di]).start()

    def z_got(a, di, h, lane, d):
        cols = cols_of(lane) if h < 4 else half_of(lane, di)
        got(AG.at[a, blk(lane, d), :, cols], z_r.at[a, di, h - 1, lane])

    def xb_send(a, d):
        ref = AG.at[a, blk(2, d), :, cols_of(2)]
        rc(ref, ref, xb_s.at[a, d % 8], xb_r.at[a, d % 8], partner).start()

    def xb_got(a, d):
        got(AG.at[a, blk(1, d), :, cols_of(2)], xb_r.at[a, d % 8])

    def ag_start(a):
        ref = AG.at[a, n_me, :, cols_of(0)]
        rc(ref, ref, xa_s.at[a], xa_r.at[a], partner).start()
        for lane in (0, 2):
            for di in range(2):
                z_send(a, di, 1, lane, 0)
        xb_send(a, 0)

    def ag_pair(a):
        got(AG.at[a, xo * 8 + z, :, cols_of(1)], xa_r.at[a])
        for di in range(2):
            z_send(a, di, 1, 1, 0)

    def ag_step(a, h):
        for lane in (0, 2, 1):
            for di, s in enumerate(SIGN):
                z_got(a, di, h, lane, -s * h)
                z_send(a, di, h + 1, lane, -s * h)
                if lane == 2:
                    xb_send(a, -s * h)

    def ag_last(a):
        for lane in (2, 0, 1):
            for di, s in enumerate(SIGN):
                z_got(a, di, 4, lane, -s * 4)
            if lane == 2:
                xb_send(a, 4)

    def ag_drain(a):
        rc(AG.at[a, 0, :, cols_of(0)], AG.at[a, 0, :, cols_of(0)], xa_s.at[a], xa_r.at[a], partner).wait_send()
        for d in range(8):
            ref = AG.at[a, 0, :, cols_of(2)]
            rc(ref, ref, xb_s.at[a, d], xb_r.at[a, d], partner).wait_send()
        for h in range(1, 5):
            for lane in range(3):
                for di in range(2):
                    ref = AG.at[a, 0, :, cols_of(lane) if h < 4 else half_of(lane, di)]
                    rc(ref, ref, z_s.at[a, di, h - 1, lane], z_r.at[a, di, h - 1, lane], nbr[di]).wait_send()

    ag_start(0)
    feature_pass(0)
    ag_pair(0)
    feature_end(0)
    ag_step(0, 1)

    wcopy_out.wait()

    def back_tile(i, _):
        m, t = lax.div(i, 6), lax.rem(i, 6)
        left = UI[0, pl.ds(m * 8, 8)].reshape(8 * B, D)
        rows = pl.ds(pl.multiple_of(t * 256, 256), 256)
        PB[pl.ds(m * 8, 8), :, rows] = dot(left, WO[rows, :], 1, 1).reshape(8, B, 256)
        return 0

    lax.fori_loop(0, 12, back_tile, 0)
    ag_step(0, 2)

    def rs_refs(di, s, lane):
        if lane < 2:
            cols = slice(None) if s else pl.ds(di * (HA // 2), HA // 2)
            return SA.at[di, s, lane, :, cols], RA.at[di, s, lane, :, cols]
        cols = slice(None) if s else pl.ds(di * (HB // 2), HB // 2)
        return SB.at[di, s, :, cols], RB.at[di, s, :, cols]

    def rs_send(di, s, lane):
        src, dst = rs_refs(di, s, lane)
        rc(src, dst, rz_s.at[di, s, lane], rz_r.at[di, s, lane], nbr[di]).start()

    def rs_got(di, s, lane):
        dst = rs_refs(di, s, lane)[1]
        got(dst, rz_r.at[di, s, lane])
        return dst[...].astype(F32)

    def part_of(lane, d):
        if lane < 2:
            return PB[blk(lane, d), :, cols_of(lane)]
        got(XBr.at[d % 8], rxb_r.at[d % 8])
        return PB[blk(lane, d), :, cols_of(2)] + XBr[d % 8].astype(F32)

    def rs_start_x():
        for d in (4, 3, 5, 2, 6, 1, 7, 0):
            XBs[d] = PB[blk(1, d), :, cols_of(2)].astype(BF)
            rc(XBs.at[d], XBr.at[d], rxb_s.at[d], rxb_r.at[d], partner).start()

    def rs_start_z(lane):
        val = part_of(lane, 4)
        for di in range(2):
            src = rs_refs(di, 0, lane)[0]
            width = (HA if lane < 2 else HB) // 2
            src[...] = val[:, di * width:(di + 1) * width].astype(BF)
            rs_send(di, 0, lane)

    def rs_step(s):
        for lane in range(3):
            for di, sg in enumerate(SIGN):
                come = rs_got(di, s, lane)
                val = part_of(lane, sg * (3 - s))
                full = rs_refs(di, s + 1, lane)[0]
                if s == 0:
                    width = val.shape[1] // 2
                    halves = [val[:, :width], val[:, width:]]
                    halves[di] = halves[di] + come
                    val = jnp.concatenate(halves, axis=1)
                else:
                    val = val + come
                full[...] = val.astype(BF)
                rs_send(di, s + 1, lane)

    def rs_last():
        other = part_of(1, 0) + rs_got(0, 3, 1) + rs_got(1, 3, 1)
        XA[0] = other.astype(BF)
        rc(XA.at[0], XA.at[1], rxa.at[0], rxa.at[1], partner).start()
        total = part_of(2, 0) + rs_got(0, 3, 2) + rs_got(1, 3, 2)
        AG[1, n_me, :, cols_of(2)] = (total * SL[:, cols_of(2)]).astype(BF)
        total = part_of(0, 0) + rs_got(0, 3, 0) + rs_got(1, 3, 0)
        got(XA.at[1], rxa.at[1])
        total = total + XA[1].astype(F32)
        AG[1, n_me, :, cols_of(0)] = (total * SL[:, cols_of(0)]).astype(BF)

    def rs_drain():
        for d in range(8):
            rc(XBs.at[d], XBr.at[d], rxb_s.at[d], rxb_r.at[d], partner).wait_send()
        rc(XA.at[0], XA.at[1], rxa.at[0], rxa.at[1], partner).wait_send()
        for s in range(4):
            for lane in range(3):
                for di in range(2):
                    src, dst = rs_refs(di, s, lane)
                    rc(src, dst, rz_s.at[di, s, lane], rz_r.at[di, s, lane], nbr[di]).wait_send()

    rs_start_x()
    rs_start_z(0)
    rs_start_z(1)
    ag_step(0, 3)
    rs_start_z(2)
    feature_pass(1)
    ag_last(0)
    rs_step(0)
    feature_end(1)
    for d in range(8):
        xb_got(0, d)

    def out_tile(t, _):
        rows = pl.ds(pl.multiple_of(t * 256, 256), 256)
        act = AG[0, :, :, rows].reshape(16 * B, 256)
        PO[rows, :] = dot(act, UI[0].reshape(16 * B, D), 0, 0).astype(BF)
        return 0

    lax.fori_loop(0, 2, out_tile, 0)
    rs_step(1)
    lax.fori_loop(2, 4, out_tile, 0)
    rs_step(2)
    lax.fori_loop(4, 6, out_tile, 0)
    ocopy_out = pltpu.make_async_copy(PO, gwout_o, o_sem.at[0])
    ocopy_out.start()
    rs_last()
    ag_start(1)
    wcopy_in.wait()
    ag_pair(1)

    offs = (0, 2, 6, 10, 14, 16)

    def blocks_of(h):
        if h in (0, 4):
            return [blk(0, h), blk(1, h)]
        return [blk(0, h), blk(0, -h), blk(1, h), blk(1, -h)]

    def gin_part(h):
        for d in sorted({h % 8, -h % 8}):
            xb_got(1, d)
        left = jnp.concatenate([AG[1, n] for n in blocks_of(h)], axis=0)
        m = offs[h + 1] - offs[h]
        slot = pl.ds(offs[h], m)
        theirs = WI[pl.ds(pl.multiple_of((1 - core) * HD, 128), HD), :]
        CS[0, slot] = dot(left, theirs, 1, 1).astype(BF).reshape(m, B, HD)
        rc(CS.at[0, slot], CS.at[1, slot], cs_s.at[h], cs_r.at[h], sib).start()
        mine = WI[pl.ds(pl.multiple_of(core * HD, 128), HD), :]
        Q[slot] = dot(left, mine, 1, 1).reshape(m, B, HD)

    def gin_send(h):
        m = offs[h + 1] - offs[h]
        slot = pl.ds(offs[h], m)
        got(CS.at[1, slot], cs_r.at[h])
        GO[slot] = (Q[slot] + CS[1, slot].astype(F32)).astype(BF)
        for i, n in enumerate(blocks_of(h)):
            at = offs[h] + i

            @pl.when(n == me_d)
            def _():
                GI[chip_d, core] = GO[at]

            @pl.when(n != me_d)
            def _():
                dev = (lax.div(n, 8), lax.rem(n, 8), col)
                rc(GO.at[at], GI.at[chip_d, core], gi_s.at[at], gi_r.at[me_d], dev).start()

    ag_step(1, 1)
    gin_part(0)
    ag_step(1, 2)
    gin_send(0)
    gin_part(1)
    ag_step(1, 3)
    gin_send(1)
    gin_part(2)
    ag_last(1)
    gin_send(2)
    gin_part(3)
    gin_part(4)
    gin_send(3)
    gin_send(4)

    def in_tile(t, _):
        cols = pl.ds(pl.multiple_of(t * 256, 256), 256)
        grad = AG[1, :, :, cols].reshape(16 * B, 256)
        PI[:, cols] = dot(UI[1].reshape(16 * B, D), grad, 0, 0).astype(BF)
        return 0

    lax.fori_loop(0, 6, in_tile, 0)
    ocopy_in = pltpu.make_async_copy(PI, gwin_o, o_sem.at[1])
    ocopy_in.start()

    def gi_wait(j, _):
        t = lax.rem(me_d + j, 16)
        got(GI.at[lax.div(t, 2), lax.rem(t, 2)], gi_r.at[t])
        return 0

    lax.fori_loop(1, 16, gi_wait, 0)
    for c in range(2):
        total = GI[0, c].astype(F32)
        for i in range(1, 8):
            total = total + GI[i, c].astype(F32)
        gin_o[:, c * HD:(c + 1) * HD] = total.astype(BF)

    for a in range(2):
        def sent(j, _):
            ref = UI.at[a, 0]
            rc(ref, ref, u_s.at[a, j], u_r.at[a, 0], sib).wait_send()
            return 0

        def passed(j, _):
            ref = UI.at[a, 0]
            rc(ref, ref, u_f.at[a, j], u_r.at[a, 0], sib).wait_send()
            return 0

        lax.fori_loop(1, 8, sent, 0)
        lax.fori_loop(0, 8, passed, 0)
        ag_drain(a)
    for k in range(2):
        @pl.when(jnp.logical_not(jnp.logical_and(dp == k, dp == xh)))
        def _():
            rc(pre.at[k], PRE.at[0], p_s.at[k], p_r.at[0], sib).wait_send()
    rs_drain()
    for h in range(5):
        slot = pl.ds(offs[h], offs[h + 1] - offs[h])
        rc(CS.at[0, slot], CS.at[1, slot], cs_s.at[h], cs_r.at[h], sib).wait_send()
        for i, n in enumerate(blocks_of(h)):
            @pl.when(n != me_d)
            def _():
                at = offs[h] + i
                rc(GO.at[at], GI.at[0, 0], gi_s.at[at], gi_r.at[0], sib).wait_send()
    ocopy_out.wait()
    ocopy_in.wait()


def body(inputs, upstream, preact, w_in, w_out):
    pre = jnp.pad(jnp.swapaxes(preact, 0, 1), ((0, 0), (0, 8), (0, 0)))
    vmem = pl.BlockSpec(memory_space=pltpu.VMEM)
    hbm = pl.BlockSpec(memory_space=pl.ANY)
    dma = pltpu.SemaphoreType.DMA
    grad_in, grad_w_in, grad_w_out = pl.pallas_call(
        kernel,
        out_shape=(
            jax.ShapeDtypeStruct((B, D), BF),
            jax.ShapeDtypeStruct((D, H), BF),
            jax.ShapeDtypeStruct((H, D), BF),
        ),
        in_specs=[vmem, vmem, vmem, hbm, hbm],
        out_specs=(vmem, hbm, hbm),
        scratch_shapes=[
            pltpu.VMEM((2, 16, B, D), BF),
            pltpu.VMEM((2, 16, B, H), BF),
            pltpu.VMEM((16, B, H), F32),
            pltpu.VMEM((D, H), BF),
            pltpu.VMEM((H, D), BF),
            pltpu.VMEM((2, 48, H), BF),
            pltpu.VMEM((B, H), F32),
            pltpu.VMEM((2, 4, 2, B, HA), BF),
            pltpu.VMEM((2, 4, 2, B, HA), BF),
            pltpu.VMEM((2, 4, B, HB), BF),
            pltpu.VMEM((2, 4, B, HB), BF),
            pltpu.VMEM((8, B, HB), BF),
            pltpu.VMEM((8, B, HB), BF),
            pltpu.VMEM((2, B, HA), BF),
            pltpu.VMEM((2, 16, B, HD), BF),
            pltpu.VMEM((16, B, HD), F32),
            pltpu.VMEM((16, B, HD), BF),
            pltpu.VMEM((8, 2, B, HD), BF),
            pltpu.VMEM((H, D), BF),
            pltpu.VMEM((D, H), BF),
            dma((2,)), dma((2,)), dma((2,)), dma((2,)),
            dma((2, 16)), dma((2, 8)), dma((2, 8)),
            dma((2, 2, 4, 3)), dma((2, 2, 4, 3)),
            dma((2,)), dma((2,)), dma((2, 8)), dma((2, 8)),
            dma((2, 4, 3)), dma((2, 4, 3)), dma((8,)), dma((8,)), dma((2,)),
            dma((5,)), dma((5,)), dma((16,)), dma((16,)),
        ],
        compiler_params=pltpu.CompilerParams(
            collective_id=0, has_side_effects=True, vmem_limit_bytes=60 * 2**20
        ),
        cost_estimate=pl.CostEstimate(
            flops=4 * 2 * 1280 * D * H, bytes_accessed=5 * 2 * D * H, transcendentals=B * H
        ),
    )(inputs, upstream, pre, w_in.reshape(D, H), w_out.reshape(H, D))
    return grad_in, grad_w_in.reshape(w_in.shape), grad_w_out.reshape(w_out.shape)


def solution(mesh):
    return jax.shard_map(
        body,
        mesh=mesh,
        in_specs=(
            P(("dp", "row"), "col"),
            P(("dp", "row"), "col"),
            P(("dp", "col"), None, "row"),
            P("col", "dp", "row"),
            P("dp", "row", "col"),
        ),
        out_specs=(P(("dp", "row"), "col"), P("col", "dp", "row"), P("dp", "row", "col")),
        check_vma=False,
    )
```

```python
import functools

import jax
import jax.numpy as jnp
from jax import lax
from jax.experimental import pallas as pl
from jax.experimental.pallas import tpu as pltpu
from jax.sharding import PartitionSpec as P

GELU_C = 0.7978845608028654
GELU_K = 0.044715
MESH = pl.DeviceIdType.MESH
BF = jnp.bfloat16
F32 = jnp.float32

B = 80
D = 768
H = 1536
CUT = (768, 768)
HA = 768
HB = H - HA
HD = D // 2
SIGN = (1, -1)


def gelu_parts(wide):
    inner = jnp.tanh(GELU_C * (wide + GELU_K * wide * wide * wide))
    active = 0.5 * wide * (1.0 + inner)
    slope = 0.5 * (1.0 + inner) + 0.5 * wide * (1.0 - inner * inner) * GELU_C * (
        1.0 + 3.0 * GELU_K * wide * wide
    )
    return active, slope


def dot(a, b, ca, cb):
    return lax.dot_general(a, b, (((ca,), (cb,)), ((), ())), preferred_element_type=F32)


def cols_of(lane, cut):
    return pl.ds(0, cut) if lane < 2 else pl.ds(cut, H - cut)


def half_of(lane, part, cut):
    start, size = (0, cut // 2) if lane < 2 else (cut, (H - cut) // 2)
    return pl.ds(start + part * size, size)


def kernel(
    inp, ups, pre, w_in, w_out,
    gin_o, gwin_o, gwout_o,
    UI, AG, PB, ACC, WI, WO, PRE, SL, RA, SA, RB, SB, XBr, XBs, XA, CS, Q, GO, GI,
    w_sem, p_r, p_s, u_r, u_s, u_f, z_r, z_s, xa_r, xa_s, xb_r, xb_s,
    rz_r, rz_s, rxb_r, rxb_s, rxa, cs_r, cs_s, gi_r, gi_s,
):
    dp, row, col = lax.axis_index("dp"), lax.axis_index("row"), lax.axis_index("col")
    y, core = lax.div(row, 2), lax.rem(row, 2)
    z, xh = lax.div(col, 2), lax.rem(col, 2)
    xo = 1 - xh
    me_d = dp * 8 + row
    chip_d = dp * 4 + y
    n_me = xh * 8 + z

    def zrel(d):
        return lax.rem(z + (d + 8), 8)

    def blk(lane, d):
        return (xo if lane == 1 else xh) * 8 + zrel(d)

    nbr = tuple((dp, row, zrel(s) * 2 + xh) for s in SIGN)
    partner = (dp, row, z * 2 + xo)
    sib = (dp, y * 2 + (1 - core), col)

    def rc(src, dst, ss, rs, dev):
        return pltpu.make_async_remote_copy(
            src_ref=src, dst_ref=dst, send_sem=ss, recv_sem=rs, device_id=dev, device_id_type=MESH
        )

    def got(ref, sem):
        pltpu.make_async_copy(ref, ref, sem).wait()

    wcopy_out = pltpu.make_async_copy(w_out, WO, w_sem.at[0])
    wcopy_in = pltpu.make_async_copy(w_in, WI, w_sem.at[1])
    wcopy_out.start()
    wcopy_in.start()

    barrier = pltpu.get_barrier_semaphore()

    def greet(dev):
        pl.semaphore_signal(barrier, inc=1, device_id=dev, device_id_type=MESH)

    def greet_group(j, _):
        t = lax.rem(me_d + j, 16)
        greet((lax.div(t, 8), lax.rem(t, 8), col))
        return 0

    lax.fori_loop(1, 16, greet_group, 0)
    greet(nbr[0])
    greet(nbr[1])
    greet(partner)
    greet((1 - dp, row, z * 2 + xo))
    UI[0, me_d] = ups[...]
    UI[1, me_d] = inp[...]
    pl.semaphore_wait(barrier, 19)

    dpp = (1 - dp, row, col)
    me_o = (1 - dp) * 8 + row

    def peer(j):
        return lax.rem(y + j, 4) * 2 + core

    def share(a, n, at):
        ref = UI.at[a, n]
        for j in range(1, 4):
            rc(ref, ref, u_s.at[a, at + j], u_r.at[a, n], (dp, peer(j), col)).start()
        rc(ref, ref, u_f.at[a, at], u_r.at[a, n], sib).start()

    def feature_start(a):
        ref = UI.at[a, me_d]
        rc(ref, ref, u_s.at[a, 0], u_r.at[a, me_d], dpp).start()
        share(a, me_d, 0)

    def feature_dp(a):
        got(UI.at[a, me_o], u_r.at[a, me_o])
        share(a, me_o, 4)

    def feature_pass(a):
        for j in range(1, 4):
            for i, g in enumerate((dp, 1 - dp)):
                n = g * 8 + peer(4 - j)
                ref = UI.at[a, n]
                got(ref, u_r.at[a, n])
                rc(ref, ref, u_f.at[a, i * 4 + j], u_r.at[a, n], sib).start()

    def feature_end(a):
        def step(j, _):
            n = j * 2 + (1 - core)
            got(UI.at[a, n], u_r.at[a, n])
            return 0

        lax.fori_loop(0, 8, step, 0)

    def feature_drain(a):
        ref = UI.at[a, 0]
        for j in (0, 1, 2, 3, 5, 6, 7):
            rc(ref, ref, u_s.at[a, j], u_r.at[a, 0], sib).wait_send()
        for j in range(8):
            rc(ref, ref, u_f.at[a, j], u_r.at[a, 0], sib).wait_send()

    for k in range(2):
        own = jnp.logical_and(dp == k, dp == xh)
        src, dst = pre.at[k], PRE.at[xh]

        @pl.when(own)
        def _():
            pltpu.make_async_copy(src, dst, p_r.at[xh]).start()

        @pl.when(jnp.logical_not(own))
        def _():
            rc(src, dst, p_s.at[k], p_r.at[xh], (k, row, z * 2 + dp)).start()

    feature_start(0)

    got(PRE.at[0], p_r.at[0])
    got(PRE.at[1], p_r.at[1])
    wide = jnp.concatenate([PRE[0].astype(F32), PRE[1].astype(F32)], axis=0)
    active, slope = gelu_parts(wide)
    AG[0, n_me] = active.astype(BF)
    SL[...] = slope

    def z_send(a, di, h, lane, d):
        cols = cols_of(lane, CUT[a]) if h < 4 else half_of(lane, di, CUT[a])
        ref = AG.at[a, blk(lane, d), :, cols]
        rc(ref, ref, z_s.at[a, di, h - 1, lane], z_r.at[a, di, h - 1, lane], nbr[di]).start()

    def z_got(a, di, h, lane, d):
        cols = cols_of(lane, CUT[a]) if h < 4 else half_of(lane, di, CUT[a])
        got(AG.at[a, blk(lane, d), :, cols], z_r.at[a, di, h - 1, lane])

    def xb_send(a, d):
        ref = AG.at[a, blk(2, d), :, cols_of(2, CUT[a])]
        rc(ref, ref, xb_s.at[a, d % 8], xb_r.at[a, d % 8], partner).start()

    def xb_got(a, d):
        got(AG.at[a, blk(1, d), :, cols_of(2, CUT[a])], xb_r.at[a, d % 8])

    def ag_start(a, lane):
        if lane == 0:
            ref = AG.at[a, n_me, :, cols_of(0, CUT[a])]
            rc(ref, ref, xa_s.at[a], xa_r.at[a], partner).start()
        for di in range(2):
            z_send(a, di, 1, lane, 0)
        if lane == 2:
            xb_send(a, 0)

    def ag_pair(a):
        got(AG.at[a, xo * 8 + z, :, cols_of(1, CUT[a])], xa_r.at[a])
        for di in range(2):
            z_send(a, di, 1, 1, 0)

    def ag_step(a, h, lanes=(0, 2, 1), take=True, pass_z=True, pass_x=True):
        for lane in lanes:
            for di, s in enumerate(SIGN):
                if take:
                    z_got(a, di, h, lane, -s * h)
                if pass_z:
                    z_send(a, di, h + 1, lane, -s * h)
                if lane == 2 and pass_x:
                    xb_send(a, -s * h)

    def ag_last(a):
        for lane in (2, 0, 1):
            for di, s in enumerate(SIGN):
                z_got(a, di, 4, lane, -s * 4)
            if lane == 2:
                xb_send(a, 4)

    def ag_drain(a):
        rc(AG.at[a, 0, :, cols_of(0, CUT[a])], AG.at[a, 0, :, cols_of(0, CUT[a])], xa_s.at[a], xa_r.at[a], partner).wait_send()
        for d in range(8):
            ref = AG.at[a, 0, :, cols_of(2, CUT[a])]
            rc(ref, ref, xb_s.at[a, d], xb_r.at[a, d], partner).wait_send()
        for h in range(1, 5):
            for lane in range(3):
                for di in range(2):
                    ref = AG.at[a, 0, :, cols_of(lane, CUT[a]) if h < 4 else half_of(lane, di, CUT[a])]
                    rc(ref, ref, z_s.at[a, di, h - 1, lane], z_r.at[a, di, h - 1, lane], nbr[di]).wait_send()

    ag_start(0, 0)
    ag_start(0, 2)
    feature_dp(0)
    ag_pair(0)
    feature_pass(0)
    ag_step(0, 1)
    feature_end(0)
    feature_start(1)
    wcopy_out.wait()

    def blocks_of(h):
        if h in (0, 4):
            return [blk(0, h), blk(1, h)]
        return [blk(0, h), blk(0, -h), blk(1, h), blk(1, -h)]

    def rows_of(n):
        return pl.ds(pl.multiple_of(n * B, 16), B)

    def back_part(h):
        blocks = blocks_of(h)
        left = jnp.concatenate([UI[0, n] for n in blocks], axis=0)

        def tile(t, _):
            cols = pl.ds(pl.multiple_of(t * 256, 256), 256)
            part = dot(left, WO[cols, :], 1, 1)
            for i, n in enumerate(blocks):
                PB[rows_of(n), cols] = part[i * B:(i + 1) * B]
            return 0

        lax.fori_loop(0, 6, tile, 0)

    def rs_refs(di, s, lane):
        if lane < 2:
            cols = slice(None) if s else pl.ds(di * (HA // 2), HA // 2)
            return SA.at[di, s, lane, :, cols], RA.at[di, s, lane, :, cols]
        cols = slice(None) if s else pl.ds(di * (HB // 2), HB // 2)
        return SB.at[di, s, :, cols], RB.at[di, s, :, cols]

    def rs_send(di, s, lane):
        src, dst = rs_refs(di, s, lane)
        rc(src, dst, rz_s.at[di, s, lane], rz_r.at[di, s, lane], nbr[di]).start()

    def rs_got(di, s, lane):
        dst = rs_refs(di, s, lane)[1]
        got(dst, rz_r.at[di, s, lane])
        return dst[...].astype(F32)

    def part_of(lane, d):
        if lane < 2:
            return PB[rows_of(blk(lane, d)), cols_of(lane, HA)]
        got(XBr.at[d % 8], rxb_r.at[d % 8])
        return PB[rows_of(blk(lane, d)), cols_of(2, HA)] + XBr[d % 8].astype(F32)

    def rs_start_x(h):
        for d in sorted({h % 8, -h % 8}):
            XBs[d] = PB[rows_of(blk(1, d)), cols_of(2, HA)].astype(BF)
            rc(XBs.at[d], XBr.at[d], rxb_s.at[d], rxb_r.at[d], partner).start()

    def rs_start_z(lane):
        val = part_of(lane, 4)
        for di in range(2):
            src = rs_refs(di, 0, lane)[0]
            width = (HA if lane < 2 else HB) // 2
            src[...] = val[:, di * width:(di + 1) * width].astype(BF)
            rs_send(di, 0, lane)

    def rs_step(s, *lanes):
        for lane in lanes:
            for di, sg in enumerate(SIGN):
                come = rs_got(di, s, lane)
                val = part_of(lane, sg * (3 - s))
                full = rs_refs(di, s + 1, lane)[0]
                if s == 0:
                    width = val.shape[1] // 2
                    halves = [val[:, :width], val[:, width:]]
                    halves[di] = halves[di] + come
                    val = jnp.concatenate(halves, axis=1)
                else:
                    val = val + come
                full[...] = val.astype(BF)
                rs_send(di, s + 1, lane)

    def rs_last_far():
        other = part_of(1, 0) + rs_got(0, 3, 1) + rs_got(1, 3, 1)
        XA[0] = other.astype(BF)
        rc(XA.at[0], XA.at[1], rxa.at[0], rxa.at[1], partner).start()

    def rs_last_near():
        total = part_of(0, 0) + rs_got(0, 3, 0) + rs_got(1, 3, 0)
        got(XA.at[1], rxa.at[1])
        total = total + XA[1].astype(F32)
        AG[1, n_me, :, cols_of(0, HA)] = (total * SL[:, cols_of(0, HA)]).astype(BF)

    def rs_last_x():
        total = part_of(2, 0) + rs_got(0, 3, 2) + rs_got(1, 3, 2)
        AG[1, n_me, :, cols_of(2, HA)] = (total * SL[:, cols_of(2, HA)]).astype(BF)

    def rs_drain():
        for d in range(8):
            rc(XBs.at[d], XBr.at[d], rxb_s.at[d], rxb_r.at[d], partner).wait_send()
        rc(XA.at[0], XA.at[1], rxa.at[0], rxa.at[1], partner).wait_send()
        for s in range(4):
            for lane in range(3):
                for di in range(2):
                    src, dst = rs_refs(di, s, lane)
                    rc(src, dst, rz_s.at[di, s, lane], rz_r.at[di, s, lane], nbr[di]).wait_send()

    def out_part(sets, first, end):
        blocks = [n for h in sets for n in blocks_of(h)]
        right = jnp.concatenate([UI[0, n] for n in blocks], axis=0)

        def tile(t, _):
            rows = pl.ds(pl.multiple_of(t * 256, 256), 256)
            left = jnp.concatenate([AG[0, n, :, rows] for n in blocks], axis=0)
            part = dot(left, right, 0, 0)
            if 4 in sets:
                gwout_o[rows, :] = (ACC[rows, :] + part).astype(BF)
            else:
                ACC[rows, :] = part
            return 0

        lax.fori_loop(first, end, tile, 0)

    def in_part(sets, first, end):
        blocks = [n for h in sets for n in blocks_of(h)]
        left = jnp.concatenate([UI[1, n] for n in blocks], axis=0)

        def tile(t, _):
            cols = pl.ds(pl.multiple_of(t * 256, 256), 256)
            right = jnp.concatenate([AG[1, n, :, cols] for n in blocks], axis=0)
            part = dot(left, right, 0, 0)
            if 4 in sets:
                gwin_o[:, cols] = (PB[:D, cols] + part).astype(BF)
            elif 0 in sets:
                PB[:D, cols] = part
            else:
                PB[:D, cols] += part
            return 0

        lax.fori_loop(first, end, tile, 0)

    offs = (0, 2, 6, 10, 14, 16)

    def gin_part(h):
        for d in sorted({h % 8, -h % 8}):
            xb_got(1, d)
        left = jnp.concatenate([AG[1, n] for n in blocks_of(h)], axis=0)
        m = offs[h + 1] - offs[h]
        slot = pl.ds(offs[h], m)
        theirs = WI[pl.ds(pl.multiple_of((1 - core) * HD, 128), HD), :]
        CS[0, slot] = dot(left, theirs, 1, 1).astype(BF).reshape(m, B, HD)
        rc(CS.at[0, slot], CS.at[1, slot], cs_s.at[h], cs_r.at[h], sib).start()
        mine = WI[pl.ds(pl.multiple_of(core * HD, 128), HD), :]
        Q[slot] = dot(left, mine, 1, 1).reshape(m, B, HD)

    def gin_send(h):
        m = offs[h + 1] - offs[h]
        slot = pl.ds(offs[h], m)
        got(CS.at[1, slot], cs_r.at[h])
        GO[slot] = (Q[slot] + CS[1, slot].astype(F32)).astype(BF)
        for i, n in enumerate(blocks_of(h)):
            at = offs[h] + i

            @pl.when(n == me_d)
            def _():
                GI[chip_d, core] = GO[at]

            @pl.when(n != me_d)
            def _():
                dev = (lax.div(n, 8), lax.rem(n, 8), col)
                rc(GO.at[at], GI.at[chip_d, core], gi_s.at[at], gi_r.at[me_d], dev).start()

    back_part(4)
    rs_start_x(4)
    rs_start_z(0)
    rs_start_z(1)
    back_part(3)
    rs_start_x(3)
    back_part(2)
    rs_start_x(2)
    back_part(1)
    rs_start_x(1)
    back_part(0)
    rs_start_x(0)
    rs_step(0, 0, 1)
    rs_start_z(2)
    feature_dp(1)
    rs_step(1, 0, 1)
    rs_step(0, 2)
    feature_pass(1)
    rs_step(2, 0, 1)
    rs_step(1, 2)
    ag_step(0, 2, (0,))
    rs_last_far()
    rs_step(2, 2)
    ag_step(0, 2, (2, 1))
    rs_last_near()
    ag_start(1, 0)
    rs_last_x()
    ag_start(1, 2)
    wcopy_in.wait()
    feature_end(1)
    feature_drain(0)
    feature_drain(1)
    rs_drain()
    ag_pair(1)
    ag_step(1, 1)
    ag_step(0, 3, pass_z=False)
    gin_part(0)
    for d in (0, 1, 7, 2, 6):
        xb_got(0, d)
    out_part((0, 1, 2), 0, 6)
    ag_step(1, 2)
    gin_send(0)
    gin_part(1)
    in_part((0, 1), 0, 6)
    ag_step(1, 3)
    ag_step(0, 3, take=False, pass_x=False)
    gin_send(1)
    gin_part(2)
    in_part((2,), 0, 6)
    ag_last(1)
    gin_send(2)
    gin_part(3)
    gin_part(4)
    ag_last(0)
    gin_send(3)
    in_part((3, 4), 0, 3)
    gin_send(4)
    in_part((3, 4), 3, 6)
    for d in (3, 5, 4):
        xb_got(0, d)
    out_part((3, 4), 0, 6)
    ag_drain(0)

    def gi_wait(j, _):
        t = lax.rem(me_d + j, 16)
        got(GI.at[lax.div(t, 2), lax.rem(t, 2)], gi_r.at[t])
        return 0

    lax.fori_loop(1, 16, gi_wait, 0)

    def gin_sum(i, _):
        rows = pl.ds(pl.multiple_of(i * 16, 16), 16)
        for c in range(2):
            total = GI[0, c, rows].astype(F32)
            for j in range(1, 8):
                total = total + GI[j, c, rows].astype(F32)
            gin_o[rows, c * HD:(c + 1) * HD] = total.astype(BF)
        return 0

    lax.fori_loop(0, 5, gin_sum, 0)

    ag_drain(1)
    for k in range(2):
        @pl.when(jnp.logical_not(jnp.logical_and(dp == k, dp == xh)))
        def _():
            rc(pre.at[k], PRE.at[0], p_s.at[k], p_r.at[0], sib).wait_send()
    for h in range(5):
        slot = pl.ds(offs[h], offs[h + 1] - offs[h])
        rc(CS.at[0, slot], CS.at[1, slot], cs_s.at[h], cs_r.at[h], sib).wait_send()
        for i, n in enumerate(blocks_of(h)):
            @pl.when(n != me_d)
            def _():
                at = offs[h] + i
                rc(GO.at[at], GI.at[0, 0], gi_s.at[at], gi_r.at[0], sib).wait_send()


def body(inputs, upstream, preact, w_in, w_out):
    pre = jnp.swapaxes(preact, 0, 1)
    vmem = pl.BlockSpec(memory_space=pltpu.VMEM)
    hbm = pl.BlockSpec(memory_space=pl.ANY)
    dma = pltpu.SemaphoreType.DMA
    grad_in, grad_w_in, grad_w_out = pl.pallas_call(
        kernel,
        out_shape=(
            jax.ShapeDtypeStruct((B, D), BF),
            pltpu.VMEM((D, H), BF),
            pltpu.VMEM((H, D), BF),
        ),
        in_specs=[vmem, vmem, vmem, hbm, hbm],
        out_specs=(vmem, vmem, vmem),
        scratch_shapes=[
            pltpu.VMEM((2, 16, B, D), BF),
            pltpu.VMEM((2, 16, B, H), BF),
            pltpu.VMEM((16 * B, H), F32),
            pltpu.VMEM((H, D), F32),
            pltpu.VMEM((D, H), BF),
            pltpu.VMEM((H, D), BF),
            pltpu.VMEM((2, 40, H), BF),
            pltpu.VMEM((B, H), F32),
            pltpu.VMEM((2, 4, 2, B, HA), BF),
            pltpu.VMEM((2, 4, 2, B, HA), BF),
            pltpu.VMEM((2, 4, B, HB), BF),
            pltpu.VMEM((2, 4, B, HB), BF),
            pltpu.VMEM((8, B, HB), BF),
            pltpu.VMEM((8, B, HB), BF),
            pltpu.VMEM((2, B, HA), BF),
            pltpu.VMEM((2, 16, B, HD), BF),
            pltpu.VMEM((16, B, HD), F32),
            pltpu.VMEM((16, B, HD), BF),
            pltpu.VMEM((8, 2, B, HD), BF),
            dma((2,)), dma((2,)), dma((2,)),
            dma((2, 16)), dma((2, 8)), dma((2, 8)),
            dma((2, 2, 4, 3)), dma((2, 2, 4, 3)),
            dma((2,)), dma((2,)), dma((2, 8)), dma((2, 8)),
            dma((2, 4, 3)), dma((2, 4, 3)), dma((8,)), dma((8,)), dma((2,)),
            dma((5,)), dma((5,)), dma((16,)), dma((16,)),
        ],
        compiler_params=pltpu.CompilerParams(
            collective_id=0, has_side_effects=True, vmem_limit_bytes=56 * 2**20
        ),
        cost_estimate=pl.CostEstimate(
            flops=4 * 2 * 1280 * D * H, bytes_accessed=5 * 2 * D * H, transcendentals=B * H
        ),
    )(inputs, upstream, pre, w_in.reshape(D, H), w_out.reshape(H, D))
    return grad_in, grad_w_in.reshape(w_in.shape), grad_w_out.reshape(w_out.shape)


def solution(mesh):
    return jax.shard_map(
        body,
        mesh=mesh,
        in_specs=(
            P(("dp", "row"), "col"),
            P(("dp", "row"), "col"),
            P(("dp", "col"), None, "row"),
            P("col", "dp", "row"),
            P("dp", "row", "col"),
        ),
        out_specs=(P(("dp", "row"), "col"), P("col", "dp", "row"), P("dp", "row", "col")),
        check_vma=False,
    )
```

```python
import functools

import jax
import jax.numpy as jnp
from jax import lax
from jax.experimental import pallas as pl
from jax.experimental.pallas import tpu as pltpu
from jax.sharding import PartitionSpec as P

GELU_C = 0.7978845608028654
GELU_K = 0.044715
MESH = pl.DeviceIdType.MESH
BF = jnp.bfloat16
F32 = jnp.float32

B = 80
D = 768
H = 1536
CUT = (768, 768)
HA = 768
HB = H - HA
HD = D // 2
SIGN = (1, -1)


def gelu_parts(wide):
    inner = jnp.tanh(GELU_C * (wide + GELU_K * wide * wide * wide))
    active = 0.5 * wide * (1.0 + inner)
    slope = 0.5 * (1.0 + inner) + 0.5 * wide * (1.0 - inner * inner) * GELU_C * (
        1.0 + 3.0 * GELU_K * wide * wide
    )
    return active, slope


def dot(a, b, ca, cb):
    return lax.dot_general(a, b, (((ca,), (cb,)), ((), ())), preferred_element_type=F32)


def cols_of(lane, cut):
    return pl.ds(0, cut) if lane < 2 else pl.ds(cut, H - cut)


def half_of(lane, part, cut):
    start, size = (0, cut // 2) if lane < 2 else (cut, (H - cut) // 2)
    return pl.ds(start + part * size, size)


def kernel(
    inp, ups, pre, w_in, w_out,
    gin_o, gwin_o, gwout_o,
    UI, AG, PB, ACC, WI, WO, PV, PK, PRE, SL, RA, SA, RB, SB, XBr, XBs, XA, CS, Q, GO, GI, RX,
    w_sem, p_r, p_s, u_r, u_s, u_f, z_r, z_s, xa_r, xa_s, xb_r, xb_s,
    rz_r, rz_s, rxb_r, rxb_s, rxa, cs_r, cs_s, gi_r, gi_s, rx_r, rx_s,
):
    dp, row, col = lax.axis_index("dp"), lax.axis_index("row"), lax.axis_index("col")
    y, core = lax.div(row, 2), lax.rem(row, 2)
    z, xh = lax.div(col, 2), lax.rem(col, 2)
    xo = 1 - xh
    me_d = dp * 8 + row
    chip_d = dp * 4 + y
    n_me = xh * 8 + z

    def zrel(d):
        return lax.rem(z + (d + 8), 8)

    def blk(lane, d):
        return (xo if lane == 1 else xh) * 8 + zrel(d)

    nbr = tuple((dp, row, zrel(s) * 2 + xh) for s in SIGN)
    partner = (dp, row, z * 2 + xo)
    sib = (dp, y * 2 + (1 - core), col)

    def rc(src, dst, ss, rs, dev):
        return pltpu.make_async_remote_copy(
            src_ref=src, dst_ref=dst, send_sem=ss, recv_sem=rs, device_id=dev, device_id_type=MESH
        )

    def got(ref, sem):
        pltpu.make_async_copy(ref, ref, sem).wait()

    wcopy_out = pltpu.make_async_copy(w_out, WO, w_sem.at[0])
    wcopy_in = pltpu.make_async_copy(w_in, WI, w_sem.at[1])

    barrier = pltpu.get_barrier_semaphore()

    def greet(dev):
        pl.semaphore_signal(barrier, inc=1, device_id=dev, device_id_type=MESH)

    def greet_group(j, _):
        t = lax.rem(me_d + j, 16)
        greet((lax.div(t, 8), lax.rem(t, 8), col))
        return 0

    lax.fori_loop(1, 16, greet_group, 0)
    greet(nbr[0])
    greet(nbr[1])
    greet(partner)
    greet((1 - dp, row, z * 2 + xo))
    own_copies = [
        pltpu.make_async_copy(ref, UI.at[a, me_d], w_sem.at[2 + a]) for a, ref in enumerate((ups, inp))
    ]
    own_copies.append(pltpu.make_async_copy(pre, PV, w_sem.at[4]))
    for copy in own_copies:
        copy.start()
    wcopy_out.start()
    wcopy_in.start()
    for copy in own_copies:
        copy.wait()
    both = PV[...]
    for k in range(2):
        PK[k] = both[:, k, :]
    pl.semaphore_wait(barrier, 19)

    dpp = (1 - dp, row, col)
    me_o = (1 - dp) * 8 + row

    def peer(j):
        return lax.rem(y + j, 4) * 2 + core

    def share(a, n, at):
        ref = UI.at[a, n]
        for j in range(1, 4):
            rc(ref, ref, u_s.at[a, at + j], u_r.at[a, n], (dp, peer(j), col)).start()
        rc(ref, ref, u_f.at[a, at], u_r.at[a, n], sib).start()

    def feature_start(a):
        ref = UI.at[a, me_d]
        rc(ref, ref, u_s.at[a, 0], u_r.at[a, me_d], dpp).start()
        share(a, me_d, 0)

    def feature_dp(a):
        got(UI.at[a, me_o], u_r.at[a, me_o])
        share(a, me_o, 4)

    def feature_pass(a):
        for j in range(1, 4):
            for i, g in enumerate((dp, 1 - dp)):
                n = g * 8 + peer(4 - j)
                ref = UI.at[a, n]
                got(ref, u_r.at[a, n])
                rc(ref, ref, u_f.at[a, i * 4 + j], u_r.at[a, n], sib).start()

    def feature_end(a):
        def step(j, _):
            n = j * 2 + (1 - core)
            got(UI.at[a, n], u_r.at[a, n])
            return 0

        lax.fori_loop(0, 8, step, 0)

    def feature_drain(a):
        ref = UI.at[a, 0]
        for j in (0, 1, 2, 3, 5, 6, 7):
            rc(ref, ref, u_s.at[a, j], u_r.at[a, 0], sib).wait_send()
        for j in range(8):
            rc(ref, ref, u_f.at[a, j], u_r.at[a, 0], sib).wait_send()

    groups = (cols_of(0, CUT[0]), cols_of(2, CUT[0]))
    for c, cols in enumerate(groups):
        for k in range(2):
            own = jnp.logical_and(dp == k, dp == xh)
            src, dst = PK.at[k, :, cols], PRE.at[xh, :, cols]

            @pl.when(own)
            def _():
                pltpu.make_async_copy(src, dst, p_r.at[c, xh]).start()

            @pl.when(jnp.logical_not(own))
            def _():
                rc(src, dst, p_s.at[c, k], p_r.at[c, xh], (k, row, z * 2 + dp)).start()

    feature_start(0)

    def act_part(c):
        cols = groups[c]
        for i in range(2):
            got(PRE.at[i, :, cols], p_r.at[c, i])
        wide = jnp.concatenate([PRE[0, :, cols].astype(F32), PRE[1, :, cols].astype(F32)], axis=0)
        active, slope = gelu_parts(wide)
        AG[0, n_me, :, cols] = active.astype(BF)
        SL[:, cols] = slope

    def z_send(a, di, h, lane, d):
        cols = cols_of(lane, CUT[a]) if h < 4 else half_of(lane, di, CUT[a])
        ref = AG.at[a, blk(lane, d), :, cols]
        rc(ref, ref, z_s.at[a, di, h - 1, lane], z_r.at[a, di, h - 1, lane], nbr[di]).start()

    def z_got(a, di, h, lane, d):
        cols = cols_of(lane, CUT[a]) if h < 4 else half_of(lane, di, CUT[a])
        got(AG.at[a, blk(lane, d), :, cols], z_r.at[a, di, h - 1, lane])

    def xb_send(a, d):
        ref = AG.at[a, blk(2, d), :, cols_of(2, CUT[a])]
        rc(ref, ref, xb_s.at[a, d % 8], xb_r.at[a, d % 8], partner).start()

    def xb_got(a, d):
        got(AG.at[a, blk(1, d), :, cols_of(2, CUT[a])], xb_r.at[a, d % 8])

    def ag_start(a, lane):
        if lane == 0:
            ref = AG.at[a, n_me, :, cols_of(0, CUT[a])]
            rc(ref, ref, xa_s.at[a], xa_r.at[a], partner).start()
        for di in range(2):
            z_send(a, di, 1, lane, 0)
        if lane == 2:
            xb_send(a, 0)

    def ag_pair(a):
        got(AG.at[a, xo * 8 + z, :, cols_of(1, CUT[a])], xa_r.at[a])
        for di in range(2):
            z_send(a, di, 1, 1, 0)

    def ag_step(a, h, lanes=(2, 0, 1), take=True, pass_z=True, pass_x=True):
        for lane in lanes:
            for di, s in enumerate(SIGN):
                if take:
                    z_got(a, di, h, lane, -s * h)
                if pass_z:
                    z_send(a, di, h + 1, lane, -s * h)
                if lane == 2 and pass_x:
                    xb_send(a, -s * h)

    def ag_last(a, lanes=(2, 0, 1)):
        for lane in lanes:
            for di, s in enumerate(SIGN):
                z_got(a, di, 4, lane, -s * 4)
            if lane == 2:
                xb_send(a, 4)

    def ag_drain(a):
        rc(AG.at[a, 0, :, cols_of(0, CUT[a])], AG.at[a, 0, :, cols_of(0, CUT[a])], xa_s.at[a], xa_r.at[a], partner).wait_send()
        for d in range(8):
            ref = AG.at[a, 0, :, cols_of(2, CUT[a])]
            rc(ref, ref, xb_s.at[a, d], xb_r.at[a, d], partner).wait_send()
        for h in range(1, 5):
            for lane in range(3):
                for di in range(2):
                    ref = AG.at[a, 0, :, cols_of(lane, CUT[a]) if h < 4 else half_of(lane, di, CUT[a])]
                    rc(ref, ref, z_s.at[a, di, h - 1, lane], z_r.at[a, di, h - 1, lane], nbr[di]).wait_send()

    act_part(0)
    ag_start(0, 0)
    act_part(1)
    ag_start(0, 2)
    feature_dp(0)
    ag_pair(0)
    ag_step(0, 1, (0,))
    feature_pass(0)
    ag_step(0, 1, (2,), pass_x=False)
    xb_send(0, -1)
    feature_end(0)
    feature_start(1)
    wcopy_out.wait()

    def blocks_of(h):
        if h in (0, 4):
            return [blk(0, h), blk(1, h)]
        return [blk(0, h), blk(0, -h), blk(1, h), blk(1, -h)]

    def rows_of(n):
        return pl.ds(pl.multiple_of(n * B, 16), B)

    def back_part(*sets):
        blocks = [n for h in sets for n in blocks_of(h)]
        left = jnp.concatenate([UI[0, n] for n in blocks], axis=0)

        def tile(t, _):
            cols = pl.ds(pl.multiple_of(t * 256, 256), 256)
            part = dot(left, WO[cols, :], 1, 1)
            for i, n in enumerate(blocks):
                PB[rows_of(n), cols] = part[i * B:(i + 1) * B]
            return 0

        lax.fori_loop(0, 6, tile, 0)

    def rs_refs(di, s, lane):
        if lane < 2:
            cols = slice(None) if s else pl.ds(di * (HA // 2), HA // 2)
            return SA.at[di, s, lane, :, cols], RA.at[di, s, lane, :, cols]
        cols = slice(None) if s else pl.ds(di * (HB // 2), HB // 2)
        return SB.at[di, s, :, cols], RB.at[di, s, :, cols]

    def rs_send(di, s, lane):
        src, dst = rs_refs(di, s, lane)
        rc(src, dst, rz_s.at[di, s, lane], rz_r.at[di, s, lane], nbr[di]).start()

    def rs_got(di, s, lane):
        dst = rs_refs(di, s, lane)[1]
        got(dst, rz_r.at[di, s, lane])
        return dst[...].astype(F32)

    def part_of(lane, d):
        if lane < 2:
            return PB[rows_of(blk(lane, d)), cols_of(lane, HA)]
        got(XBr.at[d % 8], rxb_r.at[d % 8])
        return PB[rows_of(blk(lane, d)), cols_of(2, HA)] + XBr[d % 8].astype(F32)

    def rs_start_x(h):
        for d in sorted({h % 8, -h % 8}):
            XBs[d] = PB[rows_of(blk(1, d)), cols_of(2, HA)].astype(BF)
            rc(XBs.at[d], XBr.at[d], rxb_s.at[d], rxb_r.at[d], partner).start()

    def rs_start_z(lane):
        val = part_of(lane, 4)
        for di in range(2):
            src = rs_refs(di, 0, lane)[0]
            width = (HA if lane < 2 else HB) // 2
            src[...] = val[:, di * width:(di + 1) * width].astype(BF)
            rs_send(di, 0, lane)

    def rs_step(s, *lanes):
        for lane in lanes:
            for di, sg in enumerate(SIGN):
                come = rs_got(di, s, lane)
                val = part_of(lane, sg * (3 - s))
                full = rs_refs(di, s + 1, lane)[0]
                if s == 0:
                    width = val.shape[1] // 2
                    halves = [val[:, :width], val[:, width:]]
                    halves[di] = halves[di] + come
                    val = jnp.concatenate(halves, axis=1)
                else:
                    val = val + come
                full[...] = val.astype(BF)
                rs_send(di, s + 1, lane)

    def rs_last_far():
        other = part_of(1, 0) + rs_got(0, 3, 1) + rs_got(1, 3, 1)
        XA[0] = other.astype(BF)
        rc(XA.at[0], XA.at[1], rxa.at[0], rxa.at[1], partner).start()

    def rs_last_near():
        total = part_of(0, 0) + rs_got(0, 3, 0) + rs_got(1, 3, 0)
        got(XA.at[1], rxa.at[1])
        total = total + XA[1].astype(F32)
        AG[1, n_me, :, cols_of(0, HA)] = (total * SL[:, cols_of(0, HA)]).astype(BF)

    def rs_last_x():
        total = part_of(2, 0) + rs_got(0, 3, 2) + rs_got(1, 3, 2)
        AG[1, n_me, :, cols_of(2, HA)] = (total * SL[:, cols_of(2, HA)]).astype(BF)

    def rs_drain():
        for d in range(8):
            rc(XBs.at[d], XBr.at[d], rxb_s.at[d], rxb_r.at[d], partner).wait_send()
        rc(XA.at[0], XA.at[1], rxa.at[0], rxa.at[1], partner).wait_send()
        for s in range(4):
            for lane in range(3):
                for di in range(2):
                    src, dst = rs_refs(di, s, lane)
                    rc(src, dst, rz_s.at[di, s, lane], rz_r.at[di, s, lane], nbr[di]).wait_send()

    def out_part(sets, first, end):
        blocks = [n for h in sets for n in blocks_of(h)]
        right = jnp.concatenate([UI[0, n] for n in blocks], axis=0)

        def tile(t, _):
            rows = pl.ds(pl.multiple_of(t * 256, 256), 256)
            left = jnp.concatenate([AG[0, n, :, rows] for n in blocks], axis=0)
            part = dot(left, right, 0, 0)
            if 4 in sets:
                gwout_o[rows, :] = (ACC[rows, :] + part).astype(BF)
            else:
                ACC[rows, :] = part
            return 0

        lax.fori_loop(first, end, tile, 0)

    def in_part(sets, first, end):
        blocks = [n for h in sets for n in blocks_of(h)]
        left = jnp.concatenate([UI[1, n] for n in blocks], axis=0)

        def tile(t, _):
            cols = pl.ds(pl.multiple_of(t * 256, 256), 256)
            right = jnp.concatenate([AG[1, n, :, cols] for n in blocks], axis=0)
            part = dot(left, right, 0, 0)
            if 4 in sets:
                gwin_o[:, cols] = (PB[:D, cols] + part).astype(BF)
            elif 0 in sets:
                PB[:D, cols] = part
            else:
                PB[:D, cols] += part
            return 0

        lax.fori_loop(first, end, tile, 0)

    offs = (0, 2, 6, 10, 14, 16)

    def gin_targets(h):
        targets = []
        for i, n in enumerate(blocks_of(h)):
            g, r = lax.div(n, 8), lax.rem(n, 8)
            slot = jnp.where(g == dp, 0, 1)
            to = g if h >= 3 else dp
            own = jnp.logical_and(r == row, to == dp)
            targets.append((offs[h] + i, (to, r, col), slot, own))
        return targets

    away = lax.rem(row + 8 - z, 8)
    direct = jnp.logical_and(away >= 3, away <= 5)

    def gi_wait(slot):
        def one(j, _):
            yy, c = lax.div(j, 2), lax.rem(j, 2)
            own = jnp.logical_and(j == row, jnp.logical_not(jnp.logical_and(direct, slot == 1)))

            @pl.when(jnp.logical_not(own))
            def _():
                got(GI.at[slot, yy, c], gi_r.at[slot, yy, c])

            return 0

        lax.fori_loop(0, 8, one, 0)

    def gi_rows(i, slot):
        rows = pl.ds(pl.multiple_of(i * 16, 16), 16)
        sums = []
        for c in range(2):
            total = GI[slot, 0, c, rows].astype(F32)
            for j in range(1, 4):
                total = total + GI[slot, j, c, rows].astype(F32)
            sums.append(total)
        return rows, jnp.concatenate(sums, axis=1)

    def gin_relay():
        @pl.when(jnp.logical_not(direct))
        def _():
            gi_wait(1)

            def step(i, _):
                rows, total = gi_rows(i, 1)
                RX[0, rows] = total.astype(BF)
                return 0

            lax.fori_loop(0, 5, step, 0)
            rc(RX.at[0], RX.at[1], rx_s.at[0], rx_r.at[0], dpp).start()

    def gin_final():
        gi_wait(0)

        @pl.when(direct)
        def _():
            gi_wait(1)

            def step(i, _):
                rows, total = gi_rows(i, 0)
                gin_o[rows] = (total + gi_rows(i, 1)[1]).astype(BF)
                return 0

            lax.fori_loop(0, 5, step, 0)

        @pl.when(jnp.logical_not(direct))
        def _():
            got(RX.at[1], rx_r.at[0])

            def step(i, _):
                rows, total = gi_rows(i, 0)
                gin_o[rows] = (total + RX[1, rows].astype(F32)).astype(BF)
                return 0

            lax.fori_loop(0, 5, step, 0)
            rc(RX.at[0], RX.at[1], rx_s.at[0], rx_r.at[0], dpp).wait_send()

    def gin_part(h):
        for d in sorted({h % 8, -h % 8}):
            xb_got(1, d)
        left = jnp.concatenate([AG[1, n] for n in blocks_of(h)], axis=0)
        m = offs[h + 1] - offs[h]
        slot = pl.ds(offs[h], m)
        theirs = WI[pl.ds(pl.multiple_of((1 - core) * HD, 128), HD), :]
        CS[0, slot] = dot(left, theirs, 1, 1).astype(BF).reshape(m, B, HD)
        rc(CS.at[0, slot], CS.at[1, slot], cs_s.at[h], cs_r.at[h], sib).start()
        mine = WI[pl.ds(pl.multiple_of(core * HD, 128), HD), :]
        Q[slot] = dot(left, mine, 1, 1).reshape(m, B, HD)

    def gin_send(h):
        m = offs[h + 1] - offs[h]
        slot = pl.ds(offs[h], m)
        got(CS.at[1, slot], cs_r.at[h])
        GO[slot] = (Q[slot] + CS[1, slot].astype(F32)).astype(BF)
        for at, dev, slot, own in gin_targets(h):
            @pl.when(own)
            def _():
                GI[slot, y, core] = GO[at]

            @pl.when(jnp.logical_not(own))
            def _():
                rc(GO.at[at], GI.at[slot, y, core], gi_s.at[at], gi_r.at[slot, y, core], dev).start()

    back_part(4, 3)
    rs_start_x(4)
    rs_start_z(0)
    rs_start_z(1)
    ag_step(0, 1, (1,))
    rs_start_x(3)
    back_part(2, 1, 0)
    rs_start_x(2)
    rs_step(0, 0, 1)
    rs_start_z(2)
    rs_start_x(1)
    rs_start_x(0)
    xb_send(0, 1)
    feature_dp(1)
    rs_step(1, 0, 1)
    rs_step(0, 2)
    feature_pass(1)
    rs_step(2, 0, 1)
    rs_step(1, 2)
    rs_last_far()
    rs_step(2, 2)
    ag_step(0, 2, (2,), pass_x=False)
    rs_last_near()
    ag_start(1, 0)
    rs_last_x()
    ag_start(1, 2)
    ag_step(0, 2, (2,), take=False, pass_z=False)
    wcopy_in.wait()
    feature_end(1)
    feature_drain(0)
    feature_drain(1)
    rs_drain()
    ag_pair(1)
    ag_step(1, 1)
    ag_step(0, 3, (2,))
    gin_part(0)
    for d in (0, 1, 7, 2, 6):
        xb_got(0, d)
    for di, sg in enumerate(SIGN):
        for lane in (0, 1):
            z_got(0, di, 2, lane, -sg * 2)
    out_part((0, 1, 2), 0, 6)
    ag_step(1, 2)
    gin_send(0)
    gin_part(1)
    in_part((0, 1), 0, 6)
    ag_step(1, 3)
    ag_step(0, 2, (0, 1), take=False)
    gin_send(1)
    gin_part(2)
    ag_last(1, (2,))
    ag_last(0, (2,))
    in_part((2,), 0, 6)
    ag_last(1, (0, 1))
    gin_send(2)
    gin_part(3)
    gin_part(4)
    gin_send(3)
    ag_step(0, 3, (0, 1))
    in_part((3, 4), 0, 3)
    gin_send(4)
    in_part((3, 4), 3, 6)
    gin_relay()
    for d in (3, 5, 4):
        xb_got(0, d)
    out_part((3, 4), 3, 6)
    ag_last(0, (0, 1))
    out_part((3, 4), 0, 3)
    ag_drain(0)

    gin_final()

    ag_drain(1)
    for c, cols in enumerate(groups):
        for k in range(2):
            @pl.when(jnp.logical_not(jnp.logical_and(dp == k, dp == xh)))
            def _():
                rc(PK.at[k, :, cols], PRE.at[0, :, cols], p_s.at[c, k], p_r.at[c, 0], sib).wait_send()
    for h in range(5):
        slot = pl.ds(offs[h], offs[h + 1] - offs[h])
        rc(CS.at[0, slot], CS.at[1, slot], cs_s.at[h], cs_r.at[h], sib).wait_send()
        for at, _, _, own in gin_targets(h):
            @pl.when(jnp.logical_not(own))
            def _():
                rc(GO.at[at], GI.at[0, 0, 0], gi_s.at[at], gi_r.at[0, 0, 0], sib).wait_send()


def body(inputs, upstream, preact, w_in, w_out):
    vmem = pl.BlockSpec(memory_space=pltpu.VMEM)
    hbm = pl.BlockSpec(memory_space=pl.ANY)
    dma = pltpu.SemaphoreType.DMA
    grad_in, grad_w_in, grad_w_out = pl.pallas_call(
        kernel,
        out_shape=(
            jax.ShapeDtypeStruct((B, D), BF),
            pltpu.VMEM((D, H), BF),
            pltpu.VMEM((H, D), BF),
        ),
        in_specs=[hbm, hbm, hbm, hbm, hbm],
        out_specs=(vmem, vmem, vmem),
        scratch_shapes=[
            pltpu.VMEM((2, 16, B, D), BF),
            pltpu.VMEM((2, 16, B, H), BF),
            pltpu.VMEM((16 * B, H), F32),
            pltpu.VMEM((H, D), F32),
            pltpu.VMEM((D, H), BF),
            pltpu.VMEM((H, D), BF),
            pltpu.VMEM((40, 2, H), BF),
            pltpu.VMEM((2, 40, H), BF),
            pltpu.VMEM((2, 40, H), BF),
            pltpu.VMEM((B, H), F32),
            pltpu.VMEM((2, 4, 2, B, HA), BF),
            pltpu.VMEM((2, 4, 2, B, HA), BF),
            pltpu.VMEM((2, 4, B, HB), BF),
            pltpu.VMEM((2, 4, B, HB), BF),
            pltpu.VMEM((8, B, HB), BF),
            pltpu.VMEM((8, B, HB), BF),
            pltpu.VMEM((2, B, HA), BF),
            pltpu.VMEM((2, 16, B, HD), BF),
            pltpu.VMEM((16, B, HD), F32),
            pltpu.VMEM((16, B, HD), BF),
            pltpu.VMEM((2, 4, 2, B, HD), BF),
            pltpu.VMEM((2, B, D), BF),
            dma((5,)), dma((2, 2)), dma((2, 2)),
            dma((2, 16)), dma((2, 8)), dma((2, 8)),
            dma((2, 2, 4, 3)), dma((2, 2, 4, 3)),
            dma((2,)), dma((2,)), dma((2, 8)), dma((2, 8)),
            dma((2, 4, 3)), dma((2, 4, 3)), dma((8,)), dma((8,)), dma((2,)),
            dma((5,)), dma((5,)), dma((2, 4, 2)), dma((16,)), dma((1,)), dma((1,)),
        ],
        compiler_params=pltpu.CompilerParams(
            collective_id=0, has_side_effects=True, vmem_limit_bytes=56 * 2**20
        ),
        cost_estimate=pl.CostEstimate(
            flops=4 * 2 * 1280 * D * H, bytes_accessed=5 * 2 * D * H, transcendentals=B * H
        ),
    )(inputs, upstream, preact, w_in.reshape(D, H), w_out.reshape(H, D))
    return grad_in, grad_w_in.reshape(w_in.shape), grad_w_out.reshape(w_out.shape)


def solution(mesh):
    return jax.shard_map(
        body,
        mesh=mesh,
        in_specs=(
            P(("dp", "row"), "col"),
            P(("dp", "row"), "col"),
            P(("dp", "col"), None, "row"),
            P("col", "dp", "row"),
            P("dp", "row", "col"),
        ),
        out_specs=(P(("dp", "row"), "col"), P("col", "dp", "row"), P("dp", "row", "col")),
        check_vma=False,
    )
```

```python
import functools

import jax
import jax.numpy as jnp
from jax import lax
from jax.experimental import pallas as pl
from jax.experimental.pallas import tpu as pltpu
from jax.sharding import PartitionSpec as P

GELU_C = 0.7978845608028654
GELU_K = 0.044715
MESH = pl.DeviceIdType.MESH
BF = jnp.bfloat16
F32 = jnp.float32

B = 80
D = 768
H = 1536
CUT = (768, 768)
HA = 768
HB = H - HA
HD = D // 2
SIGN = (1, -1)


def gelu_parts(wide):
    inner = jnp.tanh(GELU_C * (wide + GELU_K * wide * wide * wide))
    active = 0.5 * wide * (1.0 + inner)
    slope = 0.5 * (1.0 + inner) + 0.5 * wide * (1.0 - inner * inner) * GELU_C * (
        1.0 + 3.0 * GELU_K * wide * wide
    )
    return active, slope


def dot(a, b, ca, cb):
    return lax.dot_general(a, b, (((ca,), (cb,)), ((), ())), preferred_element_type=F32)


def cols_of(lane, cut):
    return pl.ds(0, cut) if lane < 2 else pl.ds(cut, H - cut)


def half_of(lane, part, cut):
    start, size = (0, cut // 2) if lane < 2 else (cut, (H - cut) // 2)
    return pl.ds(start + part * size, size)


def kernel(
    inp, ups, pre, w_in, w_out,
    gin_o, gwin_o, gwout_o,
    UI, AG, PB, ACC, WI, WO, PV, PK, PRE, SL, RA, SA, RB, SB, XBr, XBs, XA, CS, Q, GO, GI, RX,
    w_sem, p_r, p_s, u_r, u_s, u_f, z_r, z_s, xa_r, xa_s, xb_r, xb_s,
    rz_r, rz_s, rxb_r, rxb_s, rxa, cs_r, cs_s, gi_r, gi_s, rx_r, rx_s,
):
    dp, row, col = lax.axis_index("dp"), lax.axis_index("row"), lax.axis_index("col")
    y, core = lax.div(row, 2), lax.rem(row, 2)
    z, xh = lax.div(col, 2), lax.rem(col, 2)
    xo = 1 - xh
    me_d = dp * 8 + row
    chip_d = dp * 4 + y
    n_me = xh * 8 + z

    def zrel(d):
        return lax.rem(z + (d + 8), 8)

    def blk(lane, d):
        return (xo if lane == 1 else xh) * 8 + zrel(d)

    nbr = tuple((dp, row, zrel(s) * 2 + xh) for s in SIGN)
    partner = (dp, row, z * 2 + xo)
    sib = (dp, y * 2 + (1 - core), col)

    def rc(src, dst, ss, rs, dev):
        return pltpu.make_async_remote_copy(
            src_ref=src, dst_ref=dst, send_sem=ss, recv_sem=rs, device_id=dev, device_id_type=MESH
        )

    def got(ref, sem):
        pltpu.make_async_copy(ref, ref, sem).wait()

    wcopy_out = pltpu.make_async_copy(w_out, WO, w_sem.at[0])
    wcopy_in = pltpu.make_async_copy(w_in, WI, w_sem.at[1])

    barrier = pltpu.get_barrier_semaphore()

    def greet(dev):
        pl.semaphore_signal(barrier, inc=1, device_id=dev, device_id_type=MESH)

    def greet_group(j, _):
        t = lax.rem(me_d + j, 16)
        greet((lax.div(t, 8), lax.rem(t, 8), col))
        return 0

    lax.fori_loop(1, 16, greet_group, 0)
    greet(nbr[0])
    greet(nbr[1])
    greet(partner)
    greet((1 - dp, row, z * 2 + xo))
    own_copies = [
        pltpu.make_async_copy(ref, UI.at[a, me_d], w_sem.at[2 + a]) for a, ref in enumerate((ups, inp))
    ]
    own_copies.append(pltpu.make_async_copy(pre, PV, w_sem.at[4]))
    for copy in own_copies:
        copy.start()
    wcopy_out.start()
    wcopy_in.start()
    for copy in own_copies:
        copy.wait()
    both = PV[...]
    for k in range(2):
        PK[k] = jnp.zeros((48, H), BF)
        PK[k, :40] = both[:, k, :]
    pl.semaphore_wait(barrier, 19)

    dpp = (1 - dp, row, col)
    me_o = (1 - dp) * 8 + row

    def peer(j):
        return lax.rem(y + j, 4) * 2 + core

    def share(a, n, at):
        ref = UI.at[a, n]
        for j in range(1, 4):
            rc(ref, ref, u_s.at[a, at + j], u_r.at[a, n], (dp, peer(j), col)).start()
        rc(ref, ref, u_f.at[a, at], u_r.at[a, n], sib).start()

    def feature_start(a):
        ref = UI.at[a, me_d]
        rc(ref, ref, u_s.at[a, 0], u_r.at[a, me_d], dpp).start()
        share(a, me_d, 0)

    def feature_dp(a):
        got(UI.at[a, me_o], u_r.at[a, me_o])
        share(a, me_o, 4)

    def feature_pass(a):
        for j in range(1, 4):
            for i, g in enumerate((dp, 1 - dp)):
                n = g * 8 + peer(4 - j)
                ref = UI.at[a, n]
                got(ref, u_r.at[a, n])
                rc(ref, ref, u_f.at[a, i * 4 + j], u_r.at[a, n], sib).start()

    def feature_end(a):
        def step(j, _):
            n = j * 2 + (1 - core)
            got(UI.at[a, n], u_r.at[a, n])
            return 0

        lax.fori_loop(0, 8, step, 0)

    def feature_drain(a):
        ref = UI.at[a, 0]
        for j in (0, 1, 2, 3, 5, 6, 7):
            rc(ref, ref, u_s.at[a, j], u_r.at[a, 0], sib).wait_send()
        for j in range(8):
            rc(ref, ref, u_f.at[a, j], u_r.at[a, 0], sib).wait_send()

    groups = (cols_of(0, CUT[0]), cols_of(2, CUT[0]))
    for c, cols in enumerate(groups):
        for k in range(2):
            own = jnp.logical_and(dp == k, dp == xh)
            src, dst = PK.at[k, :, cols], PRE.at[xh, :, cols]

            @pl.when(own)
            def _():
                pltpu.make_async_copy(src, dst, p_r.at[c, xh]).start()

            @pl.when(jnp.logical_not(own))
            def _():
                rc(src, dst, p_s.at[c, k], p_r.at[c, xh], (k, row, z * 2 + dp)).start()

    feature_start(0)

    def act_part(c):
        cols = groups[c]
        for i in range(2):
            got(PRE.at[i, :, cols], p_r.at[c, i])
        wide = jnp.concatenate([PRE[0, :, cols].astype(F32)[:40], PRE[1, :, cols].astype(F32)[:40]], axis=0)
        active, slope = gelu_parts(wide)
        AG[0, n_me, :, cols] = active.astype(BF)
        SL[:, cols] = slope

    def z_send(a, di, h, lane, d):
        cols = cols_of(lane, CUT[a]) if h < 4 else half_of(lane, di, CUT[a])
        ref = AG.at[a, blk(lane, d), :, cols]
        rc(ref, ref, z_s.at[a, di, h - 1, lane], z_r.at[a, di, h - 1, lane], nbr[di]).start()

    def z_got(a, di, h, lane, d):
        cols = cols_of(lane, CUT[a]) if h < 4 else half_of(lane, di, CUT[a])
        got(AG.at[a, blk(lane, d), :, cols], z_r.at[a, di, h - 1, lane])

    def xb_send(a, d):
        ref = AG.at[a, blk(2, d), :, cols_of(2, CUT[a])]
        rc(ref, ref, xb_s.at[a, d % 8], xb_r.at[a, d % 8], partner).start()

    def xb_got(a, d):
        got(AG.at[a, blk(1, d), :, cols_of(2, CUT[a])], xb_r.at[a, d % 8])

    def ag_start(a, lane):
        if lane == 0:
            ref = AG.at[a, n_me, :, cols_of(0, CUT[a])]
            rc(ref, ref, xa_s.at[a], xa_r.at[a], partner).start()
        for di in range(2):
            z_send(a, di, 1, lane, 0)
        if lane == 2:
            xb_send(a, 0)

    def ag_pair(a):
        got(AG.at[a, xo * 8 + z, :, cols_of(1, CUT[a])], xa_r.at[a])
        for di in range(2):
            z_send(a, di, 1, 1, 0)

    def ag_step(a, h, lanes=(2, 0, 1), take=True, pass_z=True, pass_x=True):
        for lane in lanes:
            for di, s in enumerate(SIGN):
                if take:
                    z_got(a, di, h, lane, -s * h)
                if pass_z:
                    z_send(a, di, h + 1, lane, -s * h)
                if lane == 2 and pass_x:
                    xb_send(a, -s * h)

    def ag_last(a, lanes=(2, 0, 1)):
        for lane in lanes:
            for di, s in enumerate(SIGN):
                z_got(a, di, 4, lane, -s * 4)
            if lane == 2:
                xb_send(a, 4)

    def ag_drain(a):
        rc(AG.at[a, 0, :, cols_of(0, CUT[a])], AG.at[a, 0, :, cols_of(0, CUT[a])], xa_s.at[a], xa_r.at[a], partner).wait_send()
        for d in range(8):
            ref = AG.at[a, 0, :, cols_of(2, CUT[a])]
            rc(ref, ref, xb_s.at[a, d], xb_r.at[a, d], partner).wait_send()
        for h in range(1, 5):
            for lane in range(3):
                for di in range(2):
                    ref = AG.at[a, 0, :, cols_of(lane, CUT[a]) if h < 4 else half_of(lane, di, CUT[a])]
                    rc(ref, ref, z_s.at[a, di, h - 1, lane], z_r.at[a, di, h - 1, lane], nbr[di]).wait_send()

    act_part(0)
    ag_start(0, 0)
    act_part(1)
    ag_start(0, 2)
    feature_dp(0)
    ag_pair(0)
    ag_step(0, 1, (0,))
    feature_pass(0)
    ag_step(0, 1, (2,), pass_x=False)
    xb_send(0, -1)
    feature_end(0)
    feature_start(1)
    wcopy_out.wait()

    def blocks_of(h):
        if h in (0, 4):
            return [blk(0, h), blk(1, h)]
        return [blk(0, h), blk(0, -h), blk(1, h), blk(1, -h)]

    def rows_of(n):
        return pl.ds(pl.multiple_of(n * B, 16), B)

    def back_part(*sets):
        blocks = [n for h in sets for n in blocks_of(h)]
        left = jnp.concatenate([UI[0, n] for n in blocks], axis=0)

        def tile(t, _):
            cols = pl.ds(pl.multiple_of(t * 256, 256), 256)
            part = dot(left, WO[cols, :], 1, 1)
            for i, n in enumerate(blocks):
                PB[rows_of(n), cols] = part[i * B:(i + 1) * B]
            return 0

        lax.fori_loop(0, 6, tile, 0)

    def rs_refs(di, s, lane):
        if lane < 2:
            cols = slice(None) if s else pl.ds(di * (HA // 2), HA // 2)
            return SA.at[di, s, lane, :, cols], RA.at[di, s, lane, :, cols]
        cols = slice(None) if s else pl.ds(di * (HB // 2), HB // 2)
        return SB.at[di, s, :, cols], RB.at[di, s, :, cols]

    def rs_send(di, s, lane):
        src, dst = rs_refs(di, s, lane)
        rc(src, dst, rz_s.at[di, s, lane], rz_r.at[di, s, lane], nbr[di]).start()

    def rs_got(di, s, lane):
        dst = rs_refs(di, s, lane)[1]
        got(dst, rz_r.at[di, s, lane])
        return dst[...].astype(F32)

    def part_of(lane, d):
        if lane < 2:
            return PB[rows_of(blk(lane, d)), cols_of(lane, HA)]
        got(XBr.at[d % 8], rxb_r.at[d % 8])
        return PB[rows_of(blk(lane, d)), cols_of(2, HA)] + XBr[d % 8].astype(F32)

    def rs_start_x(h):
        for d in sorted({h % 8, -h % 8}):
            XBs[d] = PB[rows_of(blk(1, d)), cols_of(2, HA)].astype(BF)
            rc(XBs.at[d], XBr.at[d], rxb_s.at[d], rxb_r.at[d], partner).start()

    def rs_start_z(lane):
        val = part_of(lane, 4)
        for di in range(2):
            src = rs_refs(di, 0, lane)[0]
            width = (HA if lane < 2 else HB) // 2
            src[...] = val[:, di * width:(di + 1) * width].astype(BF)
            rs_send(di, 0, lane)

    def rs_step(s, *lanes):
        for lane in lanes:
            for di, sg in enumerate(SIGN):
                come = rs_got(di, s, lane)
                val = part_of(lane, sg * (3 - s))
                full = rs_refs(di, s + 1, lane)[0]
                if s == 0:
                    width = val.shape[1] // 2
                    halves = [val[:, :width], val[:, width:]]
                    halves[di] = halves[di] + come
                    val = jnp.concatenate(halves, axis=1)
                else:
                    val = val + come
                full[...] = val.astype(BF)
                rs_send(di, s + 1, lane)

    def rs_last_far():
        other = part_of(1, 0) + rs_got(0, 3, 1) + rs_got(1, 3, 1)
        XA[0] = other.astype(BF)
        rc(XA.at[0], XA.at[1], rxa.at[0], rxa.at[1], partner).start()

    def rs_last_near():
        total = part_of(0, 0) + rs_got(0, 3, 0) + rs_got(1, 3, 0)
        got(XA.at[1], rxa.at[1])
        total = total + XA[1].astype(F32)
        AG[1, n_me, :, cols_of(0, HA)] = (total * SL[:, cols_of(0, HA)]).astype(BF)

    def rs_last_x():
        total = part_of(2, 0) + rs_got(0, 3, 2) + rs_got(1, 3, 2)
        AG[1, n_me, :, cols_of(2, HA)] = (total * SL[:, cols_of(2, HA)]).astype(BF)

    def rs_drain():
        for d in range(8):
            rc(XBs.at[d], XBr.at[d], rxb_s.at[d], rxb_r.at[d], partner).wait_send()
        rc(XA.at[0], XA.at[1], rxa.at[0], rxa.at[1], partner).wait_send()
        for s in range(4):
            for lane in range(3):
                for di in range(2):
                    src, dst = rs_refs(di, s, lane)
                    rc(src, dst, rz_s.at[di, s, lane], rz_r.at[di, s, lane], nbr[di]).wait_send()

    def out_part(sets, first, end):
        blocks = [n for h in sets for n in blocks_of(h)]
        right = jnp.concatenate([UI[0, n] for n in blocks], axis=0)

        def tile(t, _):
            rows = pl.ds(pl.multiple_of(t * 256, 256), 256)
            left = jnp.concatenate([AG[0, n, :, rows] for n in blocks], axis=0)
            part = dot(left, right, 0, 0)
            if 4 in sets:
                gwout_o[rows, :] = (ACC[rows, :] + part).astype(BF)
            else:
                ACC[rows, :] = part
            return 0

        lax.fori_loop(first, end, tile, 0)

    def in_part(sets, first, end):
        blocks = [n for h in sets for n in blocks_of(h)]
        left = jnp.concatenate([UI[1, n] for n in blocks], axis=0)

        def tile(t, _):
            cols = pl.ds(pl.multiple_of(t * 256, 256), 256)
            right = jnp.concatenate([AG[1, n, :, cols] for n in blocks], axis=0)
            part = dot(left, right, 0, 0)
            if 4 in sets:
                gwin_o[:, cols] = (PB[:D, cols] + part).astype(BF)
            elif 0 in sets:
                PB[:D, cols] = part
            else:
                PB[:D, cols] += part
            return 0

        lax.fori_loop(first, end, tile, 0)

    offs = (0, 2, 6, 10, 14, 16)

    def gin_targets(h):
        targets = []
        for i, n in enumerate(blocks_of(h)):
            g, r = lax.div(n, 8), lax.rem(n, 8)
            slot = jnp.where(g == dp, 0, 1)
            to = g if h >= 3 else dp
            own = jnp.logical_and(r == row, to == dp)
            targets.append((offs[h] + i, (to, r, col), slot, own))
        return targets

    away = lax.rem(row + 8 - z, 8)
    direct = jnp.logical_and(away >= 3, away <= 5)

    def gi_wait(slot):
        def one(j, _):
            yy, c = lax.div(j, 2), lax.rem(j, 2)
            own = jnp.logical_and(j == row, jnp.logical_not(jnp.logical_and(direct, slot == 1)))

            @pl.when(jnp.logical_not(own))
            def _():
                got(GI.at[slot, yy, c], gi_r.at[slot, yy, c])

            return 0

        lax.fori_loop(0, 8, one, 0)

    def gi_rows(i, slot):
        rows = pl.ds(pl.multiple_of(i * 16, 16), 16)
        sums = []
        for c in range(2):
            total = GI[slot, 0, c, rows].astype(F32)
            for j in range(1, 4):
                total = total + GI[slot, j, c, rows].astype(F32)
            sums.append(total)
        return rows, jnp.concatenate(sums, axis=1)

    def gin_relay():
        @pl.when(jnp.logical_not(direct))
        def _():
            gi_wait(1)

            def step(i, _):
                rows, total = gi_rows(i, 1)
                RX[0, rows] = total.astype(BF)
                return 0

            lax.fori_loop(0, 5, step, 0)
            rc(RX.at[0], RX.at[1], rx_s.at[0], rx_r.at[0], dpp).start()

    def gin_final():
        gi_wait(0)

        @pl.when(direct)
        def _():
            gi_wait(1)

            def step(i, _):
                rows, total = gi_rows(i, 0)
                gin_o[rows] = (total + gi_rows(i, 1)[1]).astype(BF)
                return 0

            lax.fori_loop(0, 5, step, 0)

        @pl.when(jnp.logical_not(direct))
        def _():
            got(RX.at[1], rx_r.at[0])

            def step(i, _):
                rows, total = gi_rows(i, 0)
                gin_o[rows] = (total + RX[1, rows].astype(F32)).astype(BF)
                return 0

            lax.fori_loop(0, 5, step, 0)
            rc(RX.at[0], RX.at[1], rx_s.at[0], rx_r.at[0], dpp).wait_send()

    def gin_part(h):
        for d in sorted({h % 8, -h % 8}):
            xb_got(1, d)
        left = jnp.concatenate([AG[1, n] for n in blocks_of(h)], axis=0)
        m = offs[h + 1] - offs[h]
        slot = pl.ds(offs[h], m)
        theirs = WI[pl.ds(pl.multiple_of((1 - core) * HD, 128), HD), :]
        CS[0, slot] = dot(left, theirs, 1, 1).astype(BF).reshape(m, B, HD)
        rc(CS.at[0, slot], CS.at[1, slot], cs_s.at[h], cs_r.at[h], sib).start()
        mine = WI[pl.ds(pl.multiple_of(core * HD, 128), HD), :]
        Q[slot] = dot(left, mine, 1, 1).reshape(m, B, HD)

    def gin_send(h):
        m = offs[h + 1] - offs[h]
        slot = pl.ds(offs[h], m)
        got(CS.at[1, slot], cs_r.at[h])
        GO[slot] = (Q[slot] + CS[1, slot].astype(F32)).astype(BF)
        for at, dev, slot, own in gin_targets(h):
            @pl.when(own)
            def _():
                GI[slot, y, core] = GO[at]

            @pl.when(jnp.logical_not(own))
            def _():
                rc(GO.at[at], GI.at[slot, y, core], gi_s.at[at], gi_r.at[slot, y, core], dev).start()

    back_part(4, 3)
    rs_start_x(4)
    rs_start_z(0)
    rs_start_z(1)
    ag_step(0, 1, (1,))
    rs_start_x(3)
    back_part(2, 1, 0)
    rs_start_x(2)
    rs_step(0, 0, 1)
    rs_start_z(2)
    rs_start_x(1)
    rs_start_x(0)
    xb_send(0, 1)
    feature_dp(1)
    rs_step(1, 0, 1)
    rs_step(0, 2)
    feature_pass(1)
    rs_step(2, 0, 1)
    rs_step(1, 2)
    rs_last_far()
    rs_step(2, 2)
    ag_step(0, 2, (2,), pass_x=False)
    rs_last_near()
    ag_start(1, 0)
    rs_last_x()
    ag_start(1, 2)
    ag_step(0, 2, (2,), take=False, pass_z=False)
    wcopy_in.wait()
    feature_end(1)
    feature_drain(0)
    feature_drain(1)
    rs_drain()
    ag_pair(1)
    ag_step(1, 1)
    ag_step(0, 3, (2,))
    gin_part(0)
    for d in (0, 1, 7, 2, 6):
        xb_got(0, d)
    for di, sg in enumerate(SIGN):
        for lane in (0, 1):
            z_got(0, di, 2, lane, -sg * 2)
    out_part((0, 1, 2), 0, 6)
    ag_step(1, 2)
    gin_send(0)
    gin_part(1)
    ag_step(1, 3, (2,))
    in_part((0, 1), 0, 6)
    ag_step(1, 3, (0, 1))
    ag_step(0, 2, (0, 1), take=False)
    gin_send(1)
    gin_part(2)
    ag_last(1, (2,))
    ag_last(0, (2,))
    ag_last(1, (0, 1))
    gin_send(2)
    gin_part(3)
    in_part((2, 3, 4), 0, 2)
    gin_send(3)
    gin_part(4)
    ag_step(0, 3, (0, 1))
    in_part((2, 3, 4), 2, 3)
    gin_send(4)
    gin_relay()
    in_part((2, 3, 4), 3, 6)
    for d in (3, 5, 4):
        xb_got(0, d)
    out_part((3, 4), 3, 6)
    ag_last(0, (0, 1))
    out_part((3, 4), 0, 3)
    ag_drain(0)

    gin_final()

    ag_drain(1)
    for c, cols in enumerate(groups):
        for k in range(2):
            @pl.when(jnp.logical_not(jnp.logical_and(dp == k, dp == xh)))
            def _():
                rc(PK.at[k, :, cols], PRE.at[0, :, cols], p_s.at[c, k], p_r.at[c, 0], sib).wait_send()
    for h in range(5):
        slot = pl.ds(offs[h], offs[h + 1] - offs[h])
        rc(CS.at[0, slot], CS.at[1, slot], cs_s.at[h], cs_r.at[h], sib).wait_send()
        for at, _, _, own in gin_targets(h):
            @pl.when(jnp.logical_not(own))
            def _():
                rc(GO.at[at], GI.at[0, 0, 0], gi_s.at[at], gi_r.at[0, 0, 0], sib).wait_send()


def write_out(a, b, c, a_o, b_o, c_o, sems):
    copies = [
        pltpu.make_async_copy(src, dst, sems.at[i]) for i, (src, dst) in enumerate(((b, b_o), (c, c_o), (a, a_o)))
    ]
    for copy in copies:
        copy.start()
    for copy in copies:
        copy.wait()


def body(inputs, upstream, preact, w_in, w_out):
    vmem = pl.BlockSpec(memory_space=pltpu.VMEM)
    hbm = pl.BlockSpec(memory_space=pl.ANY)
    dma = pltpu.SemaphoreType.DMA
    grad_in, grad_w_in, grad_w_out = pl.pallas_call(
        kernel,
        out_shape=(
            pltpu.VMEM((B, D), BF),
            pltpu.VMEM((D, H), BF),
            pltpu.VMEM((H, D), BF),
        ),
        in_specs=[hbm, hbm, hbm, hbm, hbm],
        out_specs=(vmem, vmem, vmem),
        scratch_shapes=[
            pltpu.VMEM((2, 16, B, D), BF),
            pltpu.VMEM((2, 16, B, H), BF),
            pltpu.VMEM((16 * B, H), F32),
            pltpu.VMEM((H, D), F32),
            pltpu.VMEM((D, H), BF),
            pltpu.VMEM((H, D), BF),
            pltpu.VMEM((40, 2, H), BF),
            pltpu.VMEM((2, 48, H), BF),
            pltpu.VMEM((2, 48, H), BF),
            pltpu.VMEM((B, H), F32),
            pltpu.VMEM((2, 4, 2, B, HA), BF),
            pltpu.VMEM((2, 4, 2, B, HA), BF),
            pltpu.VMEM((2, 4, B, HB), BF),
            pltpu.VMEM((2, 4, B, HB), BF),
            pltpu.VMEM((8, B, HB), BF),
            pltpu.VMEM((8, B, HB), BF),
            pltpu.VMEM((2, B, HA), BF),
            pltpu.VMEM((2, 16, B, HD), BF),
            pltpu.VMEM((16, B, HD), F32),
            pltpu.VMEM((16, B, HD), BF),
            pltpu.VMEM((2, 4, 2, B, HD), BF),
            pltpu.VMEM((2, B, D), BF),
            dma((5,)), dma((2, 2)), dma((2, 2)),
            dma((2, 16)), dma((2, 8)), dma((2, 8)),
            dma((2, 2, 4, 3)), dma((2, 2, 4, 3)),
            dma((2,)), dma((2,)), dma((2, 8)), dma((2, 8)),
            dma((2, 4, 3)), dma((2, 4, 3)), dma((8,)), dma((8,)), dma((2,)),
            dma((5,)), dma((5,)), dma((2, 4, 2)), dma((16,)), dma((1,)), dma((1,)),
        ],
        compiler_params=pltpu.CompilerParams(
            collective_id=0, has_side_effects=True, vmem_limit_bytes=56 * 2**20
        ),
        cost_estimate=pl.CostEstimate(
            flops=4 * 2 * 1280 * D * H, bytes_accessed=5 * 2 * D * H, transcendentals=B * H
        ),
    )(inputs, upstream, preact, w_in.reshape(D, H), w_out.reshape(H, D))
    results = (grad_in, grad_w_in, grad_w_out)
    grad_in, grad_w_in, grad_w_out = pl.pallas_call(
        write_out,
        out_shape=tuple(jax.ShapeDtypeStruct(x.shape, x.dtype) for x in results),
        in_specs=[hbm] * 3,
        out_specs=(hbm,) * 3,
        scratch_shapes=[dma((3,))],
        compiler_params=pltpu.CompilerParams(vmem_limit_bytes=2**20),
    )(*(pltpu.with_memory_space_constraint(x, pltpu.VMEM) for x in results))
    return grad_in, grad_w_in.reshape(w_in.shape), grad_w_out.reshape(w_out.shape)


def solution(mesh):
    return jax.shard_map(
        body,
        mesh=mesh,
        in_specs=(
            P(("dp", "row"), "col"),
            P(("dp", "row"), "col"),
            P(("dp", "col"), None, "row"),
            P("col", "dp", "row"),
            P("dp", "row", "col"),
        ),
        out_specs=(P(("dp", "row"), "col"), P("col", "dp", "row"), P("dp", "row", "col")),
        check_vma=False,
    )
```

```python
import functools

import jax
import jax.numpy as jnp
from jax import lax
from jax.experimental import pallas as pl
from jax.experimental.pallas import tpu as pltpu
from jax.sharding import PartitionSpec as P

GELU_C = 0.7978845608028654
GELU_K = 0.044715
MESH = pl.DeviceIdType.MESH
BF = jnp.bfloat16
F32 = jnp.float32

B = 80
D = 768
H = 1536
CUT = (768, 768)
HA = 768
HB = H - HA
HD = D // 2
SIGN = (1, -1)


def gelu_parts(wide):
    inner = jnp.tanh(GELU_C * (wide + GELU_K * wide * wide * wide))
    active = 0.5 * wide * (1.0 + inner)
    slope = 0.5 * (1.0 + inner) + 0.5 * wide * (1.0 - inner * inner) * GELU_C * (
        1.0 + 3.0 * GELU_K * wide * wide
    )
    return active, slope


def dot(a, b, ca, cb):
    return lax.dot_general(a, b, (((ca,), (cb,)), ((), ())), preferred_element_type=F32)


def cols_of(lane, cut):
    return pl.ds(0, cut) if lane < 2 else pl.ds(cut, H - cut)


def half_of(lane, part, cut):
    start, size = (0, cut // 2) if lane < 2 else (cut, (H - cut) // 2)
    return pl.ds(start + part * size, size)


def kernel(
    inp, ups, pre, w_in, w_out,
    gin_o, gwin_o, gwout_o,
    UI, AG, PB, ACC, WI, WO, PV, PK, PRE, SL, RA, SA, RB, SB, XBr, XBs, XA, CS, Q, GO, GI, RX,
    w_sem, p_r, p_s, u_r, u_s, u_f, z_r, z_s, xa_r, xa_s, xb_r, xb_s,
    rz_r, rz_s, rxb_r, rxb_s, rxa, cs_r, cs_s, gi_r, gi_s, rx_r, rx_s,
):
    dp, row, col = lax.axis_index("dp"), lax.axis_index("row"), lax.axis_index("col")
    y, core = lax.div(row, 2), lax.rem(row, 2)
    z, xh = lax.div(col, 2), lax.rem(col, 2)
    xo = 1 - xh
    me_d = dp * 8 + row
    chip_d = dp * 4 + y
    n_me = xh * 8 + z

    def zrel(d):
        return lax.rem(z + (d + 8), 8)

    def blk(lane, d):
        return (xo if lane == 1 else xh) * 8 + zrel(d)

    nbr = tuple((dp, row, zrel(s) * 2 + xh) for s in SIGN)
    partner = (dp, row, z * 2 + xo)
    sib = (dp, y * 2 + (1 - core), col)

    def rc(src, dst, ss, rs, dev):
        return pltpu.make_async_remote_copy(
            src_ref=src, dst_ref=dst, send_sem=ss, recv_sem=rs, device_id=dev, device_id_type=MESH
        )

    def got(ref, sem):
        pltpu.make_async_copy(ref, ref, sem).wait()

    wcopy_out = pltpu.make_async_copy(w_out, WO, w_sem.at[0])
    wcopy_in = pltpu.make_async_copy(w_in, WI, w_sem.at[1])

    barrier = pltpu.get_barrier_semaphore()

    def greet(dev):
        pl.semaphore_signal(barrier, inc=1, device_id=dev, device_id_type=MESH)

    def greet_group(j, _):
        t = lax.rem(me_d + j, 16)
        greet((lax.div(t, 8), lax.rem(t, 8), col))
        return 0

    lax.fori_loop(1, 16, greet_group, 0)
    greet(nbr[0])
    greet(nbr[1])
    greet(partner)
    greet((1 - dp, row, z * 2 + xo))
    own_copies = [
        pltpu.make_async_copy(ref, UI.at[a, me_d], w_sem.at[2 + a]) for a, ref in enumerate((ups, inp))
    ]
    own_copies.append(pltpu.make_async_copy(pre, PV, w_sem.at[4]))
    for copy in own_copies:
        copy.start()
    wcopy_out.start()
    wcopy_in.start()
    for copy in own_copies:
        copy.wait()
    both = PV[...]
    for k in range(2):
        PK[k] = jnp.zeros((48, H), BF)
        PK[k, :40] = both[:, k, :]
    pl.semaphore_wait(barrier, 19)

    dpp = (1 - dp, row, col)
    me_o = (1 - dp) * 8 + row

    def peer(j):
        return lax.rem(y + j, 4) * 2 + core

    def share(a, n, at):
        ref = UI.at[a, n]
        for j in range(1, 4):
            rc(ref, ref, u_s.at[a, at + j], u_r.at[a, n], (dp, peer(j), col)).start()
        rc(ref, ref, u_f.at[a, at], u_r.at[a, n], sib).start()

    def feature_start(a):
        ref = UI.at[a, me_d]
        rc(ref, ref, u_s.at[a, 0], u_r.at[a, me_d], dpp).start()
        share(a, me_d, 0)

    def feature_dp(a):
        got(UI.at[a, me_o], u_r.at[a, me_o])
        share(a, me_o, 4)

    def feature_pass(a):
        for j in range(1, 4):
            for i, g in enumerate((dp, 1 - dp)):
                n = g * 8 + peer(4 - j)
                ref = UI.at[a, n]
                got(ref, u_r.at[a, n])
                rc(ref, ref, u_f.at[a, i * 4 + j], u_r.at[a, n], sib).start()

    def feature_end(a):
        def step(j, _):
            n = j * 2 + (1 - core)
            got(UI.at[a, n], u_r.at[a, n])
            return 0

        lax.fori_loop(0, 8, step, 0)

    def feature_drain(a):
        ref = UI.at[a, 0]
        for j in (0, 1, 2, 3, 5, 6, 7):
            rc(ref, ref, u_s.at[a, j], u_r.at[a, 0], sib).wait_send()
        for j in range(8):
            rc(ref, ref, u_f.at[a, j], u_r.at[a, 0], sib).wait_send()

    groups = (cols_of(0, CUT[0]), cols_of(2, CUT[0]))
    for c, cols in enumerate(groups):
        for k in range(2):
            own = jnp.logical_and(dp == k, dp == xh)
            src, dst = PK.at[k, :, cols], PRE.at[xh, :, cols]

            @pl.when(own)
            def _():
                pltpu.make_async_copy(src, dst, p_r.at[c, xh]).start()

            @pl.when(jnp.logical_not(own))
            def _():
                rc(src, dst, p_s.at[c, k], p_r.at[c, xh], (k, row, z * 2 + dp)).start()

    feature_start(0)

    def act_part(c):
        cols = groups[c]
        for i in range(2):
            got(PRE.at[i, :, cols], p_r.at[c, i])
        wide = jnp.concatenate([PRE[0, :, cols].astype(F32)[:40], PRE[1, :, cols].astype(F32)[:40]], axis=0)
        active, slope = gelu_parts(wide)
        AG[0, n_me, :, cols] = active.astype(BF)
        SL[:, cols] = slope

    def z_send(a, di, h, lane, d):
        cols = cols_of(lane, CUT[a]) if h < 4 else half_of(lane, di, CUT[a])
        ref = AG.at[a, blk(lane, d), :, cols]
        rc(ref, ref, z_s.at[a, di, h - 1, lane], z_r.at[a, di, h - 1, lane], nbr[di]).start()

    def z_got(a, di, h, lane, d):
        cols = cols_of(lane, CUT[a]) if h < 4 else half_of(lane, di, CUT[a])
        got(AG.at[a, blk(lane, d), :, cols], z_r.at[a, di, h - 1, lane])

    def xb_send(a, d):
        ref = AG.at[a, blk(2, d), :, cols_of(2, CUT[a])]
        rc(ref, ref, xb_s.at[a, d % 8], xb_r.at[a, d % 8], partner).start()

    def xb_got(a, d):
        got(AG.at[a, blk(1, d), :, cols_of(2, CUT[a])], xb_r.at[a, d % 8])

    def ag_start(a, lane):
        if lane == 0:
            ref = AG.at[a, n_me, :, cols_of(0, CUT[a])]
            rc(ref, ref, xa_s.at[a], xa_r.at[a], partner).start()
        for di in range(2):
            z_send(a, di, 1, lane, 0)
        if lane == 2:
            xb_send(a, 0)

    def ag_pair(a):
        got(AG.at[a, xo * 8 + z, :, cols_of(1, CUT[a])], xa_r.at[a])
        for di in range(2):
            z_send(a, di, 1, 1, 0)

    def ag_step(a, h, lanes=(2, 0, 1), take=True, pass_z=True, pass_x=True):
        for lane in lanes:
            for di, s in enumerate(SIGN):
                if take:
                    z_got(a, di, h, lane, -s * h)
                if pass_z:
                    z_send(a, di, h + 1, lane, -s * h)
                if lane == 2 and pass_x:
                    xb_send(a, -s * h)

    def ag_last(a, lanes=(2, 0, 1)):
        for lane in lanes:
            for di, s in enumerate(SIGN):
                z_got(a, di, 4, lane, -s * 4)
            if lane == 2:
                xb_send(a, 4)

    def ag_drain(a):
        rc(AG.at[a, 0, :, cols_of(0, CUT[a])], AG.at[a, 0, :, cols_of(0, CUT[a])], xa_s.at[a], xa_r.at[a], partner).wait_send()
        for d in range(8):
            ref = AG.at[a, 0, :, cols_of(2, CUT[a])]
            rc(ref, ref, xb_s.at[a, d], xb_r.at[a, d], partner).wait_send()
        for h in range(1, 5):
            for lane in range(3):
                for di in range(2):
                    ref = AG.at[a, 0, :, cols_of(lane, CUT[a]) if h < 4 else half_of(lane, di, CUT[a])]
                    rc(ref, ref, z_s.at[a, di, h - 1, lane], z_r.at[a, di, h - 1, lane], nbr[di]).wait_send()

    act_part(0)
    ag_start(0, 0)
    act_part(1)
    ag_start(0, 2)
    feature_dp(0)
    ag_pair(0)
    ag_step(0, 1, (0,))
    feature_pass(0)
    ag_step(0, 1, (2,), pass_x=False)
    xb_send(0, -1)
    feature_end(0)
    feature_start(1)
    wcopy_out.wait()

    def blocks_of(h):
        if h in (0, 4):
            return [blk(0, h), blk(1, h)]
        return [blk(0, h), blk(0, -h), blk(1, h), blk(1, -h)]

    def rows_of(n):
        return pl.ds(pl.multiple_of(n * B, 16), B)

    def back_part(*sets):
        blocks = [n for h in sets for n in blocks_of(h)]
        left = jnp.concatenate([UI[0, n] for n in blocks], axis=0)

        def tile(t, _):
            cols = pl.ds(pl.multiple_of(t * 256, 256), 256)
            part = dot(left, WO[cols, :], 1, 1)
            for i, n in enumerate(blocks):
                PB[rows_of(n), cols] = part[i * B:(i + 1) * B]
            return 0

        lax.fori_loop(0, 6, tile, 0)

    def rs_refs(di, s, lane):
        if lane < 2:
            cols = slice(None) if s else pl.ds(di * (HA // 2), HA // 2)
            return SA.at[di, s, lane, :, cols], RA.at[di, s, lane, :, cols]
        cols = slice(None) if s else pl.ds(di * (HB // 2), HB // 2)
        return SB.at[di, s, :, cols], RB.at[di, s, :, cols]

    def rs_send(di, s, lane):
        src, dst = rs_refs(di, s, lane)
        rc(src, dst, rz_s.at[di, s, lane], rz_r.at[di, s, lane], nbr[di]).start()

    def rs_got(di, s, lane):
        dst = rs_refs(di, s, lane)[1]
        got(dst, rz_r.at[di, s, lane])
        return dst[...].astype(F32)

    def part_of(lane, d):
        if lane < 2:
            return PB[rows_of(blk(lane, d)), cols_of(lane, HA)]
        got(XBr.at[d % 8], rxb_r.at[d % 8])
        return PB[rows_of(blk(lane, d)), cols_of(2, HA)] + XBr[d % 8].astype(F32)

    def rs_start_x(h):
        for d in sorted({h % 8, -h % 8}):
            XBs[d] = PB[rows_of(blk(1, d)), cols_of(2, HA)].astype(BF)
            rc(XBs.at[d], XBr.at[d], rxb_s.at[d], rxb_r.at[d], partner).start()

    def rs_start_z(lane):
        val = part_of(lane, 4)
        for di in range(2):
            src = rs_refs(di, 0, lane)[0]
            width = (HA if lane < 2 else HB) // 2
            src[...] = val[:, di * width:(di + 1) * width].astype(BF)
            rs_send(di, 0, lane)

    def rs_step(s, *lanes):
        for lane in lanes:
            for di, sg in enumerate(SIGN):
                come = rs_got(di, s, lane)
                val = part_of(lane, sg * (3 - s))
                full = rs_refs(di, s + 1, lane)[0]
                if s == 0:
                    width = val.shape[1] // 2
                    halves = [val[:, :width], val[:, width:]]
                    halves[di] = halves[di] + come
                    val = jnp.concatenate(halves, axis=1)
                else:
                    val = val + come
                full[...] = val.astype(BF)
                rs_send(di, s + 1, lane)

    def rs_last_far():
        other = part_of(1, 0) + rs_got(0, 3, 1) + rs_got(1, 3, 1)
        XA[0] = other.astype(BF)
        rc(XA.at[0], XA.at[1], rxa.at[0], rxa.at[1], partner).start()

    def rs_last_near():
        total = part_of(0, 0) + rs_got(0, 3, 0) + rs_got(1, 3, 0)
        got(XA.at[1], rxa.at[1])
        total = total + XA[1].astype(F32)
        AG[1, n_me, :, cols_of(0, HA)] = (total * SL[:, cols_of(0, HA)]).astype(BF)

    def rs_last_x():
        total = part_of(2, 0) + rs_got(0, 3, 2) + rs_got(1, 3, 2)
        AG[1, n_me, :, cols_of(2, HA)] = (total * SL[:, cols_of(2, HA)]).astype(BF)

    def rs_drain():
        for d in range(8):
            rc(XBs.at[d], XBr.at[d], rxb_s.at[d], rxb_r.at[d], partner).wait_send()
        rc(XA.at[0], XA.at[1], rxa.at[0], rxa.at[1], partner).wait_send()
        for s in range(4):
            for lane in range(3):
                for di in range(2):
                    src, dst = rs_refs(di, s, lane)
                    rc(src, dst, rz_s.at[di, s, lane], rz_r.at[di, s, lane], nbr[di]).wait_send()

    def out_part(sets, first, end):
        blocks = [n for h in sets for n in blocks_of(h)]
        right = jnp.concatenate([UI[0, n] for n in blocks], axis=0)

        def tile(t, _):
            rows = pl.ds(pl.multiple_of(t * 256, 256), 256)
            left = jnp.concatenate([AG[0, n, :, rows] for n in blocks], axis=0)
            part = dot(left, right, 0, 0)
            if 4 in sets:
                gwout_o[rows, :] = (ACC[rows, :] + part).astype(BF)
            else:
                ACC[rows, :] = part
            return 0

        lax.fori_loop(first, end, tile, 0)

    def in_part(sets, first, end):
        blocks = [n for h in sets for n in blocks_of(h)]
        left = jnp.concatenate([UI[1, n] for n in blocks], axis=0)

        def tile(t, _):
            cols = pl.ds(pl.multiple_of(t * 256, 256), 256)
            right = jnp.concatenate([AG[1, n, :, cols] for n in blocks], axis=0)
            part = dot(left, right, 0, 0)
            if 4 in sets:
                gwin_o[:, cols] = (PB[:D, cols] + part).astype(BF)
            elif 0 in sets:
                PB[:D, cols] = part
            else:
                PB[:D, cols] += part
            return 0

        lax.fori_loop(first, end, tile, 0)

    offs = (0, 2, 6, 10, 14, 16)

    def gin_targets(h):
        targets = []
        for i, n in enumerate(blocks_of(h)):
            g, r = lax.div(n, 8), lax.rem(n, 8)
            slot = jnp.where(g == dp, 0, 1)
            to = g if h >= 3 else dp
            own = jnp.logical_and(r == row, to == dp)
            targets.append((offs[h] + i, (to, r, col), slot, own))
        return targets

    away = lax.rem(row + 8 - z, 8)
    direct = jnp.logical_and(away >= 3, away <= 5)

    def gi_wait(slot):
        def one(j, _):
            yy, c = lax.div(j, 2), lax.rem(j, 2)
            own = jnp.logical_and(j == row, jnp.logical_not(jnp.logical_and(direct, slot == 1)))

            @pl.when(jnp.logical_not(own))
            def _():
                got(GI.at[slot, yy, c], gi_r.at[slot, yy, c])

            return 0

        lax.fori_loop(0, 8, one, 0)

    def gi_rows(i, slot):
        rows = pl.ds(pl.multiple_of(i * 16, 16), 16)
        sums = []
        for c in range(2):
            total = GI[slot, 0, c, rows].astype(F32)
            for j in range(1, 4):
                total = total + GI[slot, j, c, rows].astype(F32)
            sums.append(total)
        return rows, jnp.concatenate(sums, axis=1)

    def gin_relay():
        @pl.when(jnp.logical_not(direct))
        def _():
            gi_wait(1)

            def step(i, _):
                rows, total = gi_rows(i, 1)
                RX[0, rows] = total.astype(BF)
                return 0

            lax.fori_loop(0, 5, step, 0)
            rc(RX.at[0], RX.at[1], rx_s.at[0], rx_r.at[0], dpp).start()

    def gin_final():
        gi_wait(0)

        @pl.when(direct)
        def _():
            gi_wait(1)

            def step(i, _):
                rows, total = gi_rows(i, 0)
                gin_o[rows] = (total + gi_rows(i, 1)[1]).astype(BF)
                return 0

            lax.fori_loop(0, 5, step, 0)

        @pl.when(jnp.logical_not(direct))
        def _():
            got(RX.at[1], rx_r.at[0])

            def step(i, _):
                rows, total = gi_rows(i, 0)
                gin_o[rows] = (total + RX[1, rows].astype(F32)).astype(BF)
                return 0

            lax.fori_loop(0, 5, step, 0)
            rc(RX.at[0], RX.at[1], rx_s.at[0], rx_r.at[0], dpp).wait_send()

    def gin_part(h):
        for d in sorted({h % 8, -h % 8}):
            xb_got(1, d)
        left = jnp.concatenate([AG[1, n] for n in blocks_of(h)], axis=0)
        m = offs[h + 1] - offs[h]
        slot = pl.ds(offs[h], m)
        theirs = WI[pl.ds(pl.multiple_of((1 - core) * HD, 128), HD), :]
        CS[0, slot] = dot(left, theirs, 1, 1).astype(BF).reshape(m, B, HD)
        rc(CS.at[0, slot], CS.at[1, slot], cs_s.at[h], cs_r.at[h], sib).start()
        mine = WI[pl.ds(pl.multiple_of(core * HD, 128), HD), :]
        Q[slot] = dot(left, mine, 1, 1).reshape(m, B, HD)

    def gin_send(h):
        m = offs[h + 1] - offs[h]
        slot = pl.ds(offs[h], m)
        got(CS.at[1, slot], cs_r.at[h])
        GO[slot] = (Q[slot] + CS[1, slot].astype(F32)).astype(BF)
        for at, dev, slot, own in gin_targets(h):
            @pl.when(own)
            def _():
                GI[slot, y, core] = GO[at]

            @pl.when(jnp.logical_not(own))
            def _():
                rc(GO.at[at], GI.at[slot, y, core], gi_s.at[at], gi_r.at[slot, y, core], dev).start()

    back_part(4, 3)
    rs_start_x(4)
    rs_start_z(0)
    rs_start_z(1)
    ag_step(0, 1, (1,))
    rs_start_x(3)
    back_part(2, 1, 0)
    rs_start_x(2)
    rs_step(0, 0, 1)
    rs_start_z(2)
    rs_start_x(1)
    rs_start_x(0)
    xb_send(0, 1)
    feature_dp(1)
    rs_step(1, 0, 1)
    rs_step(0, 2)
    feature_pass(1)
    rs_step(2, 0, 1)
    rs_step(1, 2)
    rs_last_far()
    rs_step(2, 2)
    ag_step(0, 2, (2,), pass_x=False)
    rs_last_near()
    ag_start(1, 0)
    rs_last_x()
    ag_start(1, 2)
    ag_step(0, 2, (2,), take=False, pass_z=False)
    wcopy_in.wait()
    feature_end(1)
    feature_drain(0)
    feature_drain(1)
    rs_drain()
    ag_pair(1)
    ag_step(1, 1)
    ag_step(0, 3, (2,))
    gin_part(0)
    for d in (0, 1, 7, 2, 6):
        xb_got(0, d)
    for di, sg in enumerate(SIGN):
        for lane in (0, 1):
            z_got(0, di, 2, lane, -sg * 2)
    out_part((0, 1, 2), 0, 6)
    ag_step(1, 2)
    gin_send(0)
    gin_part(1)
    ag_step(1, 3, (2,))
    in_part((0, 1), 0, 6)
    ag_step(1, 3, (0, 1))
    ag_step(0, 2, (0, 1), take=False)
    gin_send(1)
    ag_last(1, (2,))
    gin_part(2)
    ag_last(0, (2,))
    ag_last(1, (0, 1))
    gin_send(2)
    gin_part(3)
    in_part((2, 3, 4), 0, 2)
    gin_send(3)
    gin_part(4)
    ag_step(0, 3, (0, 1))
    in_part((2, 3, 4), 2, 3)
    gin_send(4)
    gin_relay()
    in_part((2, 3, 4), 3, 6)
    for d in (3, 5, 4):
        xb_got(0, d)
    out_part((3, 4), 3, 6)
    ag_last(0, (0, 1))
    out_part((3, 4), 0, 3)
    ag_drain(0)

    gin_final()

    ag_drain(1)
    for c, cols in enumerate(groups):
        for k in range(2):
            @pl.when(jnp.logical_not(jnp.logical_and(dp == k, dp == xh)))
            def _():
                rc(PK.at[k, :, cols], PRE.at[0, :, cols], p_s.at[c, k], p_r.at[c, 0], sib).wait_send()
    for h in range(5):
        slot = pl.ds(offs[h], offs[h + 1] - offs[h])
        rc(CS.at[0, slot], CS.at[1, slot], cs_s.at[h], cs_r.at[h], sib).wait_send()
        for at, _, _, own in gin_targets(h):
            @pl.when(jnp.logical_not(own))
            def _():
                rc(GO.at[at], GI.at[0, 0, 0], gi_s.at[at], gi_r.at[0, 0, 0], sib).wait_send()


def write_out(a, b, c, a_o, b_o, c_o, sems):
    copies = [
        pltpu.make_async_copy(src, dst, sems.at[i]) for i, (src, dst) in enumerate(((b, b_o), (c, c_o), (a, a_o)))
    ]
    for copy in copies:
        copy.start()
    for copy in copies:
        copy.wait()


def body(inputs, upstream, preact, w_in, w_out):
    vmem = pl.BlockSpec(memory_space=pltpu.VMEM)
    hbm = pl.BlockSpec(memory_space=pl.ANY)
    dma = pltpu.SemaphoreType.DMA
    grad_in, grad_w_in, grad_w_out = pl.pallas_call(
        kernel,
        out_shape=(
            pltpu.VMEM((B, D), BF),
            pltpu.VMEM((D, H), BF),
            pltpu.VMEM((H, D), BF),
        ),
        in_specs=[hbm, hbm, hbm, hbm, hbm],
        out_specs=(vmem, vmem, vmem),
        scratch_shapes=[
            pltpu.VMEM((2, 16, B, D), BF),
            pltpu.VMEM((2, 16, B, H), BF),
            pltpu.VMEM((16 * B, H), F32),
            pltpu.VMEM((H, D), F32),
            pltpu.VMEM((D, H), BF),
            pltpu.VMEM((H, D), BF),
            pltpu.VMEM((40, 2, H), BF),
            pltpu.VMEM((2, 48, H), BF),
            pltpu.VMEM((2, 48, H), BF),
            pltpu.VMEM((B, H), F32),
            pltpu.VMEM((2, 4, 2, B, HA), BF),
            pltpu.VMEM((2, 4, 2, B, HA), BF),
            pltpu.VMEM((2, 4, B, HB), BF),
            pltpu.VMEM((2, 4, B, HB), BF),
            pltpu.VMEM((8, B, HB), BF),
            pltpu.VMEM((8, B, HB), BF),
            pltpu.VMEM((2, B, HA), BF),
            pltpu.VMEM((2, 16, B, HD), BF),
            pltpu.VMEM((16, B, HD), F32),
            pltpu.VMEM((16, B, HD), BF),
            pltpu.VMEM((2, 4, 2, B, HD), BF),
            pltpu.VMEM((2, B, D), BF),
            dma((5,)), dma((2, 2)), dma((2, 2)),
            dma((2, 16)), dma((2, 8)), dma((2, 8)),
            dma((2, 2, 4, 3)), dma((2, 2, 4, 3)),
            dma((2,)), dma((2,)), dma((2, 8)), dma((2, 8)),
            dma((2, 4, 3)), dma((2, 4, 3)), dma((8,)), dma((8,)), dma((2,)),
            dma((5,)), dma((5,)), dma((2, 4, 2)), dma((16,)), dma((1,)), dma((1,)),
        ],
        compiler_params=pltpu.CompilerParams(
            collective_id=0, has_side_effects=True, vmem_limit_bytes=56 * 2**20
        ),
        cost_estimate=pl.CostEstimate(
            flops=4 * 2 * 1280 * D * H, bytes_accessed=5 * 2 * D * H, transcendentals=B * H
        ),
    )(inputs, upstream, preact, w_in.reshape(D, H), w_out.reshape(H, D))
    results = (grad_in, grad_w_in, grad_w_out)
    grad_in, grad_w_in, grad_w_out = pl.pallas_call(
        write_out,
        out_shape=tuple(jax.ShapeDtypeStruct(x.shape, x.dtype) for x in results),
        in_specs=[hbm] * 3,
        out_specs=(hbm,) * 3,
        scratch_shapes=[dma((3,))],
        compiler_params=pltpu.CompilerParams(vmem_limit_bytes=2**20),
    )(*(pltpu.with_memory_space_constraint(x, pltpu.VMEM) for x in results))
    return grad_in, grad_w_in.reshape(w_in.shape), grad_w_out.reshape(w_out.shape)


def solution(mesh):
    return jax.shard_map(
        body,
        mesh=mesh,
        in_specs=(
            P(("dp", "row"), "col"),
            P(("dp", "row"), "col"),
            P(("dp", "col"), None, "row"),
            P("col", "dp", "row"),
            P("dp", "row", "col"),
        ),
        out_specs=(P(("dp", "row"), "col"), P("col", "dp", "row"), P("dp", "row", "col")),
        check_vma=False,
    )
```
